32 devices in a mesh: depth: 4 (over x, core), width: 8 (over z, y).
Axes of the slice: x: 2, y: 2, z: 4, core: 2. Of those that a mesh axis runs over, the one named last changes fastest.
Arguments:
- thermal_field: float32 [64, 256, 1024], P('depth', None, 'width'), may hold values from 1 to 3
- particulate_fraction: bfloat16 [64, 256, 1024], P('depth', None, 'width'), may hold values from 0 to 1
- sootiness_extinction: float32 [8], replicated, may hold values from 0.02 to 0.3
- vapour_extinction_rate: float32 [8], replicated, may hold values from 0.02 to 0.2
- planck_over_wavelength: float32 [8], replicated, may hold values from 2 to 8
- layer_sightline_position: int32 [4], replicated, may hold values from 0 to 3, each once
- picture_adjoint_seed: float32 [8, 256, 1024], P(None, ('depth', 'width')), may hold values from -6 to 6
Outputs:
- radiance: float32 [8, 256, 1024], P(None, ('depth', 'width'))
- temperature_gradient: float32 [64, 256, 1024], P('depth', None, 'width')
The draws below stay inside these ranges and needn't reach their ends.
Inputs may be any that keep to these rules, and one draw needn't show every extreme that they name: `layer_sightline_position`: each slab position occurs exactly once.
All inputs are finite; a program needn't handle non-finite values.
Results may differ from the reference program's by a relative error of at most 0.0003.
Values sent between devices are 32-bit elements; how exact they have to be, the bound alone decides.
No kernel may reach another device: no remote copies, remote signals or barrier semaphores. Data moves between devices by JAX's collectives and lax.ppermute only.
A program may use at most 192 MiB of HBM per device.

```python
import math
import jax
import jax.numpy as jnp
from jax import lax

NB = 8
CD = 16
PICTURE_HEIGHT = 256
SLABS = 4
SIGHTLINE_STEPS = 64
PICTURE_SPAN = 1024


def block_levels(own_key, extent, pieces, low, largest):
    loudness = 1.0
    for dim, blocks in pieces:
        steps = jax.random.uniform(jax.random.fold_in(jax.random.fold_in(own_key, 6), dim), (blocks,), jnp.float32, low / len(pieces), largest / len(pieces))
        loudness = loudness * jnp.repeat(jnp.exp(steps), extent[dim] // blocks).reshape((-1,) + (1,) * (len(extent) - 1 - dim))
    return loudness


def gaussian(own_key, dims, deviation, limit, shards=(), kind=jnp.bfloat16):
    entries = deviation * jax.random.normal(own_key, dims, jnp.float32)
    if shards:
        entries = entries * block_levels(own_key, dims, shards, -0.22, 0.18)
    return jnp.clip(entries, -limit, limit).astype(kind)


def setup_inputs(seed: int = 0) -> dict:
    arg_keys = jax.random.split(jax.random.key(seed), 8)
    thermal_field = jnp.clip(1.0 + 2.0 * jax.random.uniform(arg_keys[0], (SIGHTLINE_STEPS, PICTURE_HEIGHT, PICTURE_SPAN), jnp.float32) ** block_levels(arg_keys[0], (SIGHTLINE_STEPS, PICTURE_HEIGHT, PICTURE_SPAN), ((0, 4), (2, 8)), -0.2, 0.2), 1.0, 3.0)
    particulate_fraction = jnp.clip(1.0 * jax.random.uniform(arg_keys[1], (SIGHTLINE_STEPS, PICTURE_HEIGHT, PICTURE_SPAN), jnp.float32) ** block_levels(arg_keys[1], (SIGHTLINE_STEPS, PICTURE_HEIGHT, PICTURE_SPAN), ((0, 4), (2, 8)), -0.2, 0.2), 0.0, 1.0).astype(jnp.bfloat16)
    sootiness_extinction = jnp.clip(jnp.exp(jax.random.uniform(arg_keys[2], (NB,), jnp.float32, math.log(0.02), math.log(0.3))), 0.02, 0.3)
    vapour_extinction_rate = jnp.clip(jnp.exp(jax.random.uniform(arg_keys[3], (NB,), jnp.float32, math.log(0.02), math.log(0.2))), 0.02, 0.2)
    planck_over_wavelength = jnp.clip(jnp.exp(jax.random.uniform(arg_keys[4], (NB,), jnp.float32, math.log(2.0), math.log(8.0))), 2.0, 8.0)
    layer_sightline_position = jax.random.permutation(arg_keys[5], SLABS).astype(jnp.int32)
    picture_adjoint_seed = gaussian(arg_keys[6], (NB, PICTURE_HEIGHT, PICTURE_SPAN), 1.0, 6.0, ((1, 32),), jnp.float32)
    return dict(thermal_field=thermal_field, particulate_fraction=particulate_fraction, sootiness_extinction=sootiness_extinction, vapour_extinction_rate=vapour_extinction_rate, planck_over_wavelength=planck_over_wavelength, layer_sightline_position=layer_sightline_position, picture_adjoint_seed=picture_adjoint_seed)


precise = lax.Precision.HIGHEST


def spectral_fields(absolute_heat_level, particulate_field, particulate_multiplier, vapour_multiplier, spectral_multiplier, below_diagonal_matrix):
    sightline_length = absolute_heat_level.shape[1]
    extinction_integral = (particulate_multiplier * particulate_field + vapour_multiplier * absolute_heat_level) / sightline_length
    optical_before = jnp.einsum('kl,slq->skq', below_diagonal_matrix, extinction_integral, precision=precise)
    dimming_factor = jnp.exp(-optical_before)
    blocking_share = 1.0 - jnp.exp(-extinction_integral)
    planck_exponential = jnp.exp(spectral_multiplier / absolute_heat_level)
    emitter_term = (jnp.exp(0.5 * spectral_multiplier) - 1.0) / (planck_exponential - 1.0)
    emitter_derivative = emitter_term * planck_exponential / (planck_exponential - 1.0) * spectral_multiplier / (absolute_heat_level * absolute_heat_level)
    return extinction_integral, dimming_factor, blocking_share, emitter_term, emitter_derivative


def compose(lights, depths, order):
    in_front = (order[:, None] < order[None, :]).astype(jnp.float32)
    lies_behind = order[:, None] > order[None, :]
    optical_before = jnp.einsum('jq,js->sq', depths, in_front, precision=precise)
    dimming_factor = jnp.exp(-optical_before)
    radiance = jnp.sum(dimming_factor * lights, axis=0)
    spacing = optical_before[:, None, :] - optical_before[None, :, :] - depths[None, :, :]
    behind_mask = lies_behind[:, :, None]
    weight = jnp.where(behind_mask, jnp.exp(-jnp.where(behind_mask, spacing, 0.0)), 0.0)
    behind_light = jnp.sum(weight * lights[:, None, :], axis=0)
    return radiance, dimming_factor, behind_light


def reference(thermal_field, particulate_fraction, sootiness_extinction, vapour_extinction_rate, planck_over_wavelength, layer_sightline_position, picture_adjoint_seed):
    layer_total = SLABS
    sightline_length = CD
    picture_entries = PICTURE_HEIGHT * PICTURE_SPAN
    absolute_heat_level = thermal_field.reshape(layer_total, sightline_length, picture_entries)
    particulate_field = particulate_fraction.astype(jnp.float32).reshape(layer_total, sightline_length, picture_entries)
    below_diagonal_matrix = jnp.tril(jnp.ones((sightline_length, sightline_length), jnp.float32), -1)
    strict_upper = below_diagonal_matrix.T
    cotangent = picture_adjoint_seed.reshape(NB, picture_entries)

    def march_band(gradient, inputs):
        particulate_multiplier, vapour_multiplier, spectral_multiplier, tangent = inputs
        extinction_integral, dimming_factor, blocking_share, emitter_term, emitter_derivative = spectral_fields(absolute_heat_level, particulate_field, particulate_multiplier, vapour_multiplier, spectral_multiplier, below_diagonal_matrix)
        emitted = dimming_factor * blocking_share * emitter_term
        lights = jnp.sum(emitted, axis=1)
        depths = jnp.sum(extinction_integral, axis=1)
        radiance, front_fade, behind_light = compose(lights, depths, layer_sightline_position)
        seen_weight = tangent[None, :] * front_fade
        far_weight = seen_weight * behind_light
        emitted_after = jnp.einsum('kl,slq->skq', strict_upper, emitted, precision=precise)
        gas_rate = vapour_multiplier / sightline_length
        addend = seen_weight[:, None, :] * (dimming_factor * blocking_share * emitter_derivative + (dimming_factor * jnp.exp(-extinction_integral) * emitter_term - emitted_after) * gas_rate) - (far_weight * jnp.exp(-depths))[:, None, :] * gas_rate
        return gradient + addend, radiance

    gradient, radiance = lax.scan(march_band, jnp.zeros((layer_total, sightline_length, picture_entries), jnp.float32), (sootiness_extinction, vapour_extinction_rate, planck_over_wavelength, cotangent))
    return radiance.reshape(NB, PICTURE_HEIGHT, PICTURE_SPAN), gradient.reshape(SIGHTLINE_STEPS, PICTURE_HEIGHT, PICTURE_SPAN)
```

```python
import functools

import jax
import jax.numpy as jnp
from jax import lax
from jax.experimental import pallas as pl
from jax.experimental.pallas import tpu as pltpu
from jax.sharding import PartitionSpec as P

LOG2E = 1.4426950408889634
ROWS = 8
F32 = jnp.float32


def smem():
    return pl.BlockSpec(memory_space=pltpu.SMEM)


def vmem():
    return pl.BlockSpec(memory_space=pltpu.VMEM)


def cost(microseconds):
    return pl.CostEstimate(flops=0, bytes_accessed=int(microseconds * 3.0e6), transcendentals=0)


def params(mebibytes):
    return pltpu.CompilerParams(vmem_limit_bytes=mebibytes << 20)


def path_sums(thermal, soot_share, block):
    cells, rows, columns = thermal.shape

    def kernel(thermal_ref, soot_ref, sums_ref):
        def tile(i, _):
            here = pl.ds(pl.multiple_of(i * 2 * ROWS, 2 * ROWS), 2 * ROWS)
            soot = soot_ref[0, here].astype(F32)
            heat = thermal_ref[0, here]
            for k in range(1, cells):
                soot = soot + soot_ref[k, here].astype(F32)
                heat = heat + thermal_ref[k, here]
            sums_ref[0, here] = soot
            sums_ref[1, here] = heat
            return 0

        lax.fori_loop(0, block // (2 * ROWS), tile, 0)

    volume = pl.BlockSpec((cells, block, columns), lambda i: (0, i, 0))
    return pl.pallas_call(
        kernel,
        grid=(rows // block,),
        in_specs=[volume, volume],
        out_specs=pl.BlockSpec((2, block, columns), lambda i: (0, i, 0)),
        out_shape=jax.ShapeDtypeStruct((2, rows, columns), F32),
        compiler_params=params(8),
        cost_estimate=cost(2),
        name="path_sums",
    )(thermal, soot_share)


def march(thermal, soot_share, soot_rate, gas_rate, planck, block):
    cells, rows, columns = thermal.shape
    bands = soot_rate.shape[0]

    def kernel(soot_rate_ref, gas_rate_ref, planck_ref, thermal_ref, soot_ref, part_ref, light_ref):
        step = pl.program_id(0)

        def tile(i, _):
            here = pl.ds(pl.multiple_of(i * 2 * ROWS, 2 * ROWS), 2 * ROWS)
            soot_scale = [soot_rate_ref[b] * (-LOG2E / cells) for b in range(bands)]
            gas_scale = [gas_rate_ref[b] * (-LOG2E / cells) for b in range(bands)]
            planck_scale = [planck_ref[b] * LOG2E for b in range(bands)]
            ratio = [
                jnp.full((2 * ROWS, columns), planck_ref[b], F32)
                / jnp.full((2 * ROWS, columns), gas_rate_ref[b] * (1.0 / cells), F32)
                for b in range(bands)
            ]
            clear = [None] * bands
            light = [None] * bands
            group = step * (block // ROWS) + 2 * i
            for k in range(cells):
                heat = thermal_ref[k, here]
                soot = soot_ref[k, here].astype(F32)
                cold = 1.0 / heat
                cold2 = cold * cold
                for b in range(bands):
                    fade = jnp.exp2(soot * soot_scale[b] + heat * gas_scale[b])
                    source = pltpu.reciprocal(jnp.exp2(cold * planck_scale[b]) - 1.0, approx=True)
                    if k == 0:
                        beyond = fade
                        emitted = (1.0 - fade) * source
                        local = source
                    else:
                        beyond = clear[b] * fade
                        emitted = (clear[b] - beyond) * source
                        local = clear[b] * source + light[b]
                    part = (emitted + emitted * source) * (cold2 * ratio[b]) + local
                    part_ref[group, k, b] = part[:ROWS]
                    part_ref[group + 1, k, b] = part[ROWS:]
                    light[b] = emitted if k == 0 else light[b] + emitted
                    clear[b] = beyond
            for b in range(bands):
                light_ref[2 * i, b] = light[b][:ROWS]
                light_ref[2 * i + 1, b] = light[b][ROWS:]
            return 0

        lax.fori_loop(0, block // (2 * ROWS), tile, 0)

    volume = pl.BlockSpec((cells, block, columns), lambda i: (0, i, 0))
    return pl.pallas_call(
        kernel,
        grid=(rows // block,),
        in_specs=[smem(), smem(), smem(), volume, volume],
        out_specs=[
            vmem(),
            pl.BlockSpec((block // ROWS, bands, ROWS, columns), lambda i: (i, 0, 0, 0)),
        ],
        out_shape=[
            pltpu.VMEM((rows // ROWS, cells, bands, ROWS, columns), F32),
            jax.ShapeDtypeStruct((rows // ROWS, bands, ROWS, columns), F32),
        ],
        compiler_params=params(16),
        cost_estimate=cost(12),
        name="march",
    )(soot_rate, gas_rate, planck, thermal, soot_share)


def dim(cells, soot_rate, gas_rate, planck, order, me, sums, light):
    groups, bands, _, columns = light.shape
    slabs = order.shape[0]
    share = groups // slabs

    def kernel(soot_ref, gas_ref, planck_ref, order_ref, me_ref, *refs):
        sum_refs, (light_ref, odd_ref, even_ref, prior_ref) = refs[: slabs - 1], refs[slabs - 1 :]
        mine = me_ref[0]
        front = [
            jnp.where(order_ref[mine ^ o] < order_ref[mine], 1.0, 0.0).astype(F32)
            for o in range(1, slabs)
        ]
        scale = [jnp.exp(jnp.full((ROWS, columns), planck_ref[b] * 0.5, F32)) - 1.0 for b in range(bands)]
        for o in range(slabs):
            target = odd_ref if o % 2 else even_ref

            def tile(g, _, o=o, target=target):
                group = (mine ^ o) * share + g
                here = pl.ds(pl.multiple_of(group * ROWS, ROWS), ROWS)
                soot = sum_refs[0][0, here] * front[0]
                heat = sum_refs[0][1, here] * front[0]
                for j in range(1, slabs - 1):
                    soot = soot + sum_refs[j][0, here] * front[j]
                    heat = heat + sum_refs[j][1, here] * front[j]
                prior_ref[0, here] = soot
                prior_ref[1, here] = heat
                for b in range(bands):
                    seen = jnp.exp2(
                        soot * (soot_ref[b] * (-LOG2E / cells)) + heat * (gas_ref[b] * (-LOG2E / cells))
                    )
                    target[o // 2, g, b] = light_ref[group, b] * seen * scale[b]
                return 0

            lax.fori_loop(0, share, tile, 0)

    half = jax.ShapeDtypeStruct((slabs // 2, share, bands, ROWS, columns), F32)
    return pl.pallas_call(
        kernel,
        in_specs=[smem()] * 5 + [vmem()] * slabs,
        out_specs=[vmem()] * 3,
        out_shape=[half, half, jax.ShapeDtypeStruct((2, groups * ROWS, columns), F32)],
        compiler_params=params(16),
        cost_estimate=cost(1.5),
        name="dim",
    )(soot_rate, gas_rate, planck, order, me, *sums, light)


def pull(cells, gas_rate, me, odd, even, tangents):
    half, share, bands, _, columns = odd.shape
    slabs = 2 * half

    def kernel(gas_ref, me_ref, odd_ref, even_ref, *refs):
        tangent_refs, pull_ref = refs[:slabs], refs[slabs]
        for o in range(slabs):
            seen_ref = odd_ref if o % 2 else even_ref

            def tile(g, _, o=o, seen_ref=seen_ref):
                total = None
                for b in range(bands):
                    term = tangent_refs[o][g, b] * seen_ref[o // 2, g, b] * (gas_ref[b] * (1.0 / cells))
                    total = term if total is None else total + term
                start = ((me_ref[0] ^ o) * share + g) * ROWS
                pull_ref[pl.ds(pl.multiple_of(start, ROWS), ROWS)] = total
                return 0

            lax.fori_loop(0, share, tile, 0)

    return pl.pallas_call(
        kernel,
        in_specs=[smem()] * 2 + [vmem()] * (2 + slabs),
        out_specs=vmem(),
        out_shape=jax.ShapeDtypeStruct((slabs * share * ROWS, columns), F32),
        compiler_params=params(16),
        cost_estimate=cost(1),
        name="pull",
    )(gas_rate, me, odd, even, *tangents)


def blend(soot_rate, gas_rate, planck, order, me, prior, tangents, pulls, parts):
    groups, cells, bands, _, columns = parts.shape
    slabs = order.shape[0]
    share = groups // slabs

    def kernel(soot_ref, gas_ref, planck_ref, order_ref, me_ref, prior_ref, *refs):
        tangent_refs, pull_refs = refs[:slabs], refs[slabs : 2 * slabs]
        part_ref, out_ref = refs[2 * slabs :]
        step = pl.program_id(0)
        mine = me_ref[0]
        behind = [
            jnp.where(order_ref[mine ^ o] >= order_ref[mine], 1.0, 0.0).astype(F32) for o in range(slabs)
        ]
        scale = [
            (jnp.exp(jnp.full((ROWS, columns), planck_ref[b] * 0.5, F32)) - 1.0)
            * (gas_ref[b] * (1.0 / cells))
            for b in range(bands)
        ]
        for o in range(slabs):

            @pl.when((mine ^ o) == step)
            def _(o=o):
                def tile(g, _):
                    group = step * share + g
                    here = pl.ds(pl.multiple_of(group * ROWS, ROWS), ROWS)
                    local = pl.ds(pl.multiple_of(g * ROWS, ROWS), ROWS)
                    soot = prior_ref[0, here]
                    heat = prior_ref[1, here]
                    weight = [
                        tangent_refs[o][g, b]
                        * jnp.exp2(
                            soot * (soot_ref[b] * (-LOG2E / cells)) + heat * (gas_ref[b] * (-LOG2E / cells))
                        )
                        * scale[b]
                        for b in range(bands)
                    ]
                    away = pull_refs[0][here] * behind[0]
                    for j in range(1, slabs):
                        away = away + pull_refs[j][here] * behind[j]
                    for k in range(cells):
                        total = part_ref[group, k, 0] * weight[0] - away
                        for b in range(1, bands):
                            total = total + part_ref[group, k, b] * weight[b]
                        out_ref[k, local] = total
                    return 0

                lax.fori_loop(0, share, tile, 0)

    return pl.pallas_call(
        kernel,
        grid=(slabs,),
        in_specs=[smem()] * 5 + [vmem()] * (2 + 2 * slabs),
        out_specs=pl.BlockSpec((cells, share * ROWS, columns), lambda i: (0, i, 0)),
        out_shape=jax.ShapeDtypeStruct((cells, groups * ROWS, columns), F32),
        compiler_params=params(16),
        cost_estimate=cost(3),
        name="blend",
    )(soot_rate, gas_rate, planck, order, me, prior, *tangents, *pulls, parts)


def to_tiles(blocks):
    sources, bands, rows, columns = blocks.shape
    if rows == ROWS:
        return blocks
    lines = blocks.transpose(1, 0, 2, 3).reshape(bands, sources * rows // ROWS, ROWS, columns)
    return lines.transpose(1, 0, 2, 3)


def to_blocks(tiles, rows):
    count, bands, _, columns = tiles.shape
    if rows == ROWS:
        return tiles
    lines = tiles.transpose(1, 0, 2, 3).reshape(bands, count * ROWS // rows, rows, columns)
    return lines.transpose(1, 0, 2, 3)


def solution(mesh):
    slabs = mesh.shape["depth"]
    widths = mesh.shape["width"]
    bits = [1 << i for i in range(slabs.bit_length() - 1)]

    def swap(value, bit):
        return lax.ppermute(value, "depth", [(i, i ^ bit) for i in range(slabs)])

    def spread(value):
        pieces = {0: value}
        for bit in reversed(bits):
            for o in list(pieces):
                pieces[o ^ bit] = swap(pieces[o], bit)
        return [pieces[o] for o in range(slabs)]

    def on_device(thermal, soot_share, soot_rate, gas_rate, planck, order, seed):
        cells, rows, columns = thermal.shape
        bands, lines, _ = seed.shape
        me = lax.axis_index("depth").astype(jnp.int32).reshape(1)

        sums = spread(path_sums(thermal, soot_share, rows // 4))
        cut = seed.reshape(bands, lines, widths, columns).transpose(2, 0, 1, 3)
        tangent = to_tiles(lax.all_to_all(cut, "width", split_axis=0, concat_axis=0, tiled=True))
        tangents = spread(tangent)
        parts, light = march(thermal, soot_share, soot_rate, gas_rate, planck, rows // 8)

        odd, even, prior = dim(cells, soot_rate, gas_rate, planck, order, me, sums[1:], light)
        arrived = swap(odd, 1)
        kept = {2 * i: even[i] + arrived[i] for i in range(slabs // 2)}
        for bit in bits[1:]:
            for o in [o for o in kept if o & bit]:
                kept[o ^ bit] = kept[o ^ bit] + swap(kept.pop(o), bit)
        image = to_blocks(kept[0], lines)
        image = lax.all_to_all(image, "width", split_axis=0, concat_axis=0, tiled=True)
        image = image.transpose(1, 2, 0, 3).reshape(bands, lines, widths * columns)

        pulls = spread(pull(cells, gas_rate, me, odd, even, tangents))
        gradient = blend(soot_rate, gas_rate, planck, order, me, prior, tangents, pulls, parts)
        return image, gradient

    placed = (
        P("depth", None, "width"),
        P("depth", None, "width"),
        P(),
        P(),
        P(),
        P(),
        P(None, ("depth", "width"), None),
    )
    return jax.shard_map(
        on_device,
        mesh=mesh,
        in_specs=placed,
        out_specs=(P(None, ("depth", "width"), None), P("depth", None, "width")),
        check_vma=False,
    )
```

```python
import functools

import jax
import jax.numpy as jnp
from jax import lax
from jax.experimental import pallas as pl
from jax.experimental.pallas import tpu as pltpu
from jax.sharding import PartitionSpec as P

LOG2E = 1.4426950408889634
ROWS = 8
FLOPS_A_US = 1e9
FAR_US, NEAR_US, PULL_US, BLEND_US = 2.4, 0.1, 4, 2.4
COPIES = 8
F32 = jnp.float32

SOOT_STEP, GAS_STEP, PLANCK_STEP, SOURCE, GAS, RATIO = range(6)
KINDS = 6


def smem():
    return pl.BlockSpec(memory_space=pltpu.SMEM)


def vmem():
    return pl.BlockSpec(memory_space=pltpu.VMEM)


def hbm():
    return pl.BlockSpec(memory_space=pltpu.HBM)


def shape(*dims):
    return jax.ShapeDtypeStruct(dims, F32)


def kernel_call(body, name, in_specs, out_specs, out_shape, us=0, mebibytes=4, scratch=()):
    def held(spec):
        return spec.memory_space == pltpu.VMEM

    def placed(spec, out):
        return pltpu.VMEM(out.shape, out.dtype) if held(spec) else out

    if isinstance(out_specs, list):
        out_shape = [placed(spec, out) for spec, out in zip(out_specs, out_shape)]
    else:
        out_shape = placed(out_specs, out_shape)
    def run(*operands, ties=()):
        def untied(*refs):
            return body(*refs[: len(in_specs)], *refs[len(in_specs) + len(ties) :])

        call = pl.pallas_call(
            untied,
            in_specs=[*in_specs, *[pl.BlockSpec(memory_space=pl.ANY)] * len(ties)],
            out_specs=out_specs,
            out_shape=out_shape,
            scratch_shapes=scratch,
            compiler_params=pltpu.CompilerParams(vmem_limit_bytes=mebibytes << 20),
            cost_estimate=pl.CostEstimate(
                flops=int(us * FLOPS_A_US), bytes_accessed=1 << 20, transcendentals=0
            ),
            name=name,
        )
        return call(
            *[
                pltpu.with_memory_space_constraint(x, pltpu.VMEM) if held(spec) else x
                for spec, x in zip(in_specs, operands)
            ],
            *ties,
        )

    return run


def rows_at(tile, count=1):
    return pl.ds(pl.multiple_of(tile * ROWS, count * ROWS), count * ROWS)


def load(soot_rate, gas_rate, planck, order, thermal, soot_share, seed, widths):
    cells, rows, columns = thermal.shape
    bands, lines, _ = seed.shape
    slabs = order.shape[0]
    half = rows // 2
    step = cells // COPIES

    def kernel(
        soot_rate_ref, gas_rate_ref, planck_ref, order_ref, thermal_hbm, soot_hbm, seed_hbm,
        thermal_ref, soot_ref, near_ref, far_ref, const_ref, *cut_refs,
    ):
        *cut_refs, sems = cut_refs
        mine = lax.axis_index("depth")
        copies = []
        for o in range(widths):
            start = pl.multiple_of((lax.axis_index("width") ^ o) * columns, columns)
            copies.append((seed_hbm.at[:, :, pl.ds(start, columns)], cut_refs[o // 2].at[o % 2]))
        for i in range(COPIES):
            part = pl.ds(i * step, step)
            copies.append((thermal_hbm.at[part], thermal_ref.at[part]))
            copies.append((soot_hbm.at[part], soot_ref.at[part]))
        copies = [pltpu.make_async_copy(a, b, sems.at[i]) for i, (a, b) in enumerate(copies)]
        for copy in copies:
            copy.start()

        def tile(value):
            return jnp.full((ROWS, columns), value, F32)

        for b in range(bands):
            gas = tile(gas_rate_ref[b]) * (1.0 / cells)
            wave = tile(planck_ref[b])
            const_ref[SOOT_STEP * bands + b] = tile(soot_rate_ref[b]) * (-LOG2E / cells)
            const_ref[GAS_STEP * bands + b] = gas * -LOG2E
            const_ref[PLANCK_STEP * bands + b] = wave * LOG2E
            const_ref[SOURCE * bands + b] = jnp.exp(wave * 0.5) - 1.0
            const_ref[GAS * bands + b] = gas
            const_ref[RATIO * bands + b] = wave / gas
        for o in range(slabs):
            front = jnp.where(order_ref[mine ^ o] < order_ref[mine], 1.0, 0.0).astype(F32)
            const_ref[KINDS * bands + o] = tile(front)
            const_ref[KINDS * bands + slabs + o] = tile(1.0 - front)
        for copy in copies:
            copy.wait()
        top = mine // (slabs // 2)
        for sums_ref, first in ((near_ref, top), (far_ref, 1 - top)):

            def add(i, _, sums_ref=sums_ref, first=first):
                here = rows_at(first * (half // ROWS) + 2 * i, 2)
                soot = soot_ref[0, here].astype(F32)
                heat = thermal_ref[0, here]
                for k in range(1, cells):
                    soot = soot + soot_ref[k, here].astype(F32)
                    heat = heat + thermal_ref[k, here]
                sums_ref[0, rows_at(2 * i, 2)] = soot
                sums_ref[1, rows_at(2 * i, 2)] = heat
                return 0

            lax.fori_loop(0, half // (2 * ROWS), add, 0)

    return kernel_call(
        kernel,
        "load",
        [smem()] * 4 + [hbm()] * 3,
        [vmem()] * (5 + widths // 2),
        [
            pltpu.VMEM(thermal.shape, thermal.dtype),
            pltpu.VMEM(soot_share.shape, soot_share.dtype),
            shape(2, half, columns),
            shape(2, half, columns),
            shape(KINDS * bands + 2 * slabs, ROWS, columns),
            *[shape(2, bands, lines, columns)] * (widths // 2),
        ],
        us=0,
        mebibytes=52,
        scratch=[pltpu.SemaphoreType.DMA((2 * COPIES + widths,))],
    )(soot_rate, gas_rate, planck, order, thermal, soot_share, seed)


def march(consts, thermal, soot_share, bands, share, o, ties, us):
    cells, _, columns = thermal.shape

    def kernel(const_ref, thermal_ref, soot_ref, part_ref, light_ref):
        first = (lax.axis_index("depth") ^ o) * share

        def tile(i, _):
            here = rows_at(first + 2 * i, 2)

            def const(kind, b):
                one = const_ref[kind * bands + b]
                return jnp.concatenate([one, one], axis=0)

            clear = [None] * bands
            light = [None] * bands
            for k in range(cells):
                heat = thermal_ref[k, here]
                soot = soot_ref[k, here].astype(F32)
                cold = pltpu.reciprocal(heat, approx=True)
                cold2 = cold * cold
                for b in range(bands):
                    fade = jnp.exp2(soot * const(SOOT_STEP, b) + heat * const(GAS_STEP, b))
                    source = pltpu.reciprocal(jnp.exp2(cold * const(PLANCK_STEP, b)) - 1.0, approx=True)
                    if k == 0:
                        beyond = fade
                        emitted = (1.0 - fade) * source
                        local = source
                    else:
                        beyond = clear[b] * fade
                        emitted = (clear[b] - beyond) * source
                        local = clear[b] * source + light[b]
                    part = (emitted + emitted * source) * (cold2 * const(RATIO, b)) + local
                    part_ref[2 * i, k, b] = part[:ROWS]
                    part_ref[2 * i + 1, k, b] = part[ROWS:]
                    light[b] = emitted if k == 0 else light[b] + emitted
                    clear[b] = beyond
            for b in range(bands):
                light_ref[2 * i, b] = light[b][:ROWS]
                light_ref[2 * i + 1, b] = light[b][ROWS:]
            return 0

        lax.fori_loop(0, share // 2, tile, 0)

    return kernel_call(
        kernel,
        "march",
        [vmem()] * 3,
        [vmem()] * 2,
        [shape(share, cells, bands, ROWS, columns), shape(share, bands, ROWS, columns)],
        us=us,
    )(consts, thermal, soot_share, ties=ties)


def turn(sources, targets, ties=()):
    arrays, names = zip(*sources)
    at = {o: (i, j) for i, held in enumerate(names) for j, o in enumerate(held)}

    def kernel(*refs):
        for target, held in zip(refs[len(arrays) :], targets):
            for j, o in enumerate(held):
                target[j] = refs[at[o][0]][at[o][1]]

    return kernel_call(
        kernel,
        "turn",
        [vmem()] * len(arrays),
        [vmem()] * len(targets),
        [shape(len(held), *arrays[0].shape[1:]) for held in targets],
    )(*arrays, ties=ties)


def join(*terms, ties=()):
    blocks, bands, lines, columns = terms[0].shape

    def kernel(*refs):
        for o in range(blocks):
            total = refs[0][o]
            for ref in refs[1 : len(terms)]:
                total = total + ref[o]
            refs[len(terms) + o % 2][o // 2] = total

    return kernel_call(
        kernel,
        "join",
        [vmem()] * len(terms),
        [vmem()] * 2,
        [shape(blocks // 2, bands, lines, columns)] * 2,
    )(*terms, ties=ties)


def dim(consts, sums, lights, slabs, twisted, ties):
    share, bands, _, columns = lights[0].shape
    half = len(lights)

    def kernel(const_ref, *refs):
        sum_refs, light_refs = refs[: slabs - 1], refs[slabs - 1 : slabs - 1 + half]
        scale_refs, seen_refs = refs[-2 * half : -half], refs[-half:]
        twist = lax.axis_index("width") if twisted else 0
        for i in range(half):

            def tile(g, _, i=i):
                here = rows_at(((lax.axis_index("depth") ^ i) & (half - 1)) * share + g)
                soot = heat = 0.0
                for j in range(1, slabs):
                    front = const_ref[KINDS * bands + j]
                    soot = soot + sum_refs[j - 1][0, here] * front
                    heat = heat + sum_refs[j - 1][1, here] * front
                for b in range(bands):
                    path = soot * const_ref[SOOT_STEP * bands + b] + heat * const_ref[GAS_STEP * bands + b]
                    scale = const_ref[SOURCE * bands + b] * jnp.exp2(path)
                    scale_refs[i][g, b] = scale
                    seen_refs[i][g ^ twist, b] = light_refs[i][g, b] * scale
                return 0

            lax.fori_loop(0, share, tile, 0)

    outs = kernel_call(
        kernel,
        "dim",
        [vmem()] * (slabs + half),
        [vmem()] * (2 * half),
        [shape(share, bands, ROWS, columns)] * (2 * half),
        us=0,
    )(consts, *sums, *lights, ties=ties)
    return outs[:half], outs[half:]


def pull(consts, seen, tangents, twisted, ties=()):
    slabs = len(seen)
    share, bands, _, columns = seen[0].shape
    half = slabs // 2

    def kernel(const_ref, *refs):
        seen_refs, tangent_refs, pull_ref = refs[:slabs], refs[slabs : 2 * slabs], refs[2 * slabs]
        twist = lax.axis_index("width") if twisted else 0
        for o in range(slabs):

            def tile(i, _, o=o):
                total = None
                for b in range(bands):
                    term = tangent_refs[o][i, b] * seen_refs[o][i, b] * const_ref[GAS * bands + b]
                    total = term if total is None else total + term
                here = rows_at(((lax.axis_index("depth") ^ o) & (half - 1)) * share + (i ^ twist))
                pull_ref[o // half, here] = total
                return 0

            lax.fori_loop(0, share, tile, 0)

    return kernel_call(
        kernel,
        "pull",
        [vmem()] * (1 + 2 * slabs),
        vmem(),
        shape(2, half * share * ROWS, columns),
        us=PULL_US,
    )(consts, *seen, *tangents, ties=ties)


def blend(consts, scales, tangents, pulls, parts, twisted, ties=()):
    slabs = len(parts)
    share, cells, bands, _, columns = parts[0].shape
    half = slabs // 2

    def kernel(const_ref, *refs):
        scale_refs, tangent_refs, pull_refs, part_refs = (
            refs[i * slabs : (i + 1) * slabs] for i in range(4)
        )
        out_hbm, token_ref, gradient_ref, sems = refs[4 * slabs :]
        token_ref[...] = jnp.zeros_like(token_ref)
        mine = lax.axis_index("depth")
        twist = lax.axis_index("width") if twisted else 0
        copies = []
        for o in range(slabs):

            def tile(g, _, o=o):
                here = rows_at(((mine ^ o) & (half - 1)) * share + g)
                weight = [
                    tangent_refs[o][g ^ twist, b] * scale_refs[o][g, b] * const_ref[GAS * bands + b]
                    for b in range(bands)
                ]
                away = None
                for j in range(slabs):
                    side = (o // half) ^ (j // half)
                    term = pull_refs[j][side, here] * const_ref[KINDS * bands + slabs + j]
                    away = term if away is None else away + term
                for k in range(cells):
                    total = part_refs[o][g, k, 0] * weight[0] - away
                    for b in range(1, bands):
                        total = total + part_refs[o][g, k, b] * weight[b]
                    gradient_ref[o, k, rows_at(g)] = total
                return 0

            lax.fori_loop(0, share, tile, 0)
            rows = rows_at((mine ^ o) * share, share)
            copies.append(pltpu.make_async_copy(gradient_ref.at[o], out_hbm.at[:, rows], sems.at[o]))
            copies[-1].start()
        for copy in copies:
            copy.wait()

    height = share * ROWS
    return kernel_call(
        kernel,
        "blend",
        [vmem()] * (1 + 4 * slabs),
        [hbm(), vmem()],
        [shape(cells, slabs * height, columns), shape(ROWS, columns)],
        us=BLEND_US,
        mebibytes=8,
        scratch=[pltpu.VMEM((slabs, cells, height, columns), F32), pltpu.SemaphoreType.DMA((slabs,))],
    )(consts, *scales, *tangents, *pulls, *parts, ties=ties)


def picture(sources, ties=()):
    arrays, names = zip(*sources)
    _, bands, lines, columns = arrays[0].shape
    count = sum(len(held) for held in names)

    def kernel(*refs):
        *block_refs, out_hbm, sems = refs
        copies = []
        for ref, held in zip(block_refs, names):
            for j, o in enumerate(held):
                start = pl.multiple_of((lax.axis_index("width") ^ o) * columns, columns)
                target = out_hbm.at[:, :, pl.ds(start, columns)]
                copies.append(pltpu.make_async_copy(ref.at[j], target, sems.at[o]))
                copies[-1].start()
        for copy in copies:
            copy.wait()

    return kernel_call(
        kernel,
        "picture",
        [vmem()] * len(arrays),
        hbm(),
        shape(bands, lines, count * columns),
        scratch=[pltpu.SemaphoreType.DMA((count,))],
    )(*arrays, ties=ties)


def solution(mesh):
    slabs = mesh.shape["depth"]
    widths = mesh.shape["width"]
    top = slabs // 2
    lower_bits = [1 << i for i in range(top.bit_length() - 1)]
    near, far = range(top), range(top, slabs)

    def swap(value, bit, axis="depth"):
        pairs = [(i, i ^ bit) for i in range(mesh.shape[axis])]
        return lax.ppermute(value, axis, pairs)

    def spread(piece, across=False):
        pieces = {top if across else 0: piece}
        for bit in reversed(lower_bits):
            for o in list(pieces):
                pieces[o ^ bit] = swap(pieces[o], bit)
        return pieces

    def lower(seen):
        kept = dict(enumerate(seen))
        for bit in lower_bits:
            for o in [o for o in kept if o & bit]:
                arrived = swap(kept.pop(o), bit)
                if bit == lower_bits[-1]:
                    return kept[0], arrived
                kept[o ^ bit] = kept[o ^ bit] + arrived

    def on_device(thermal, soot_share, soot_rate, gas_rate, planck, order, seed):
        cells, rows, columns = thermal.shape
        bands, lines, _ = seed.shape
        share = rows // slabs // ROWS
        whole = lines == ROWS

        def twist(blocks):
            at = lax.axis_index("width")
            return jnp.stack([lax.dynamic_index_in_dim(blocks, at ^ o, keepdims=False) for o in range(widths)])

        def to_tiles(blocks):
            if whole:
                return blocks
            lined = twist(blocks).transpose(1, 0, 2, 3).reshape(bands, share, ROWS, columns)
            return lined.transpose(1, 0, 2, 3)

        def to_blocks(*terms, ties=()):
            if whole:
                return join(*terms, ties=ties)
            lined = sum(terms).transpose(1, 0, 2, 3).reshape(bands, widths, lines, columns)
            blocks = twist(lined.transpose(1, 0, 2, 3))
            return blocks[0::2], blocks[1::2]

        parts, lights, scales, seen = {}, {}, {}, {}

        def lit(o, us, *ties):
            parts[o], lights[o] = march(consts, heat, soot, bands, share, o, ties, us)
            return lights[o]

        def dimmed(shares, paths, *ties):
            some = dim(
                consts, [paths[j] for j in range(1, slabs)], [lights[o] for o in shares], slabs, whole, ties
            )
            for i, o in enumerate(shares):
                scales[o], seen[o] = some[0][i], some[1][i]

        evens, odds = range(0, widths, 2), range(1, widths, 2)
        groups = [(o, o + 1) for o in evens]

        def swap_groups(arrays):
            return [arrays[0], *(swap(x, g[0], "width") for x, g in zip(arrays[1:], groups[1:]))]

        heat, soot, near_sums, far_sums, consts, *cut = load(
            soot_rate, gas_rate, planck, order, thermal, soot_share, seed, widths
        )
        across_far = swap(near_sums, top)
        across_near = swap(far_sums, top)
        cut = swap_groups(cut)
        far_paths = spread(far_sums) | spread(across_far, True)
        done = lit(far[0], FAR_US)
        even, odd = turn(list(zip(cut, groups)), [evens, odds], (done,))
        odd = swap(odd, 1, "width")
        for o in far[1:]:
            done = lit(o, FAR_US, even, done)
        dimmed(far, far_paths, done)
        (blocks,) = turn([(even, evens), (odd, odds)], [range(widths)], (seen[far[0]], across_near))
        tangent = to_tiles(blocks)
        tangents = spread(tangent)
        tangent_across = swap(tangent, top)
        near_paths = spread(near_sums) | spread(across_near, True)
        seen_far = sum(lower([seen[o] for o in far]))
        across = swap(seen_far, top)
        done = tangent
        for o in near:
            done = lit(o, NEAR_US, seen_far, done)
        (tangent_across,) = turn([(tangent_across, range(share))], [range(share)], (done,))
        dimmed(near, near_paths, tangent_across)
        tangents |= spread(tangent_across, True)
        seen_near = lower([seen[o] for o in near])
        (across,) = turn([(across, range(share))], [range(share)], (seen[near[0]],))
        pulled = pull(
            consts, [seen[o] for o in range(slabs)], [tangents[o] for o in range(slabs)], whole, (across,)
        )
        pulls = spread(pulled) | spread(swap(pulled, top), True)
        image = to_blocks(*seen_near, across, ties=(pulled,))
        image = turn([(image[0], evens), (swap(image[1], 1, "width"), odds)], groups)
        image = swap_groups(image)
        gradient, done = blend(
            consts,
            *([some[o] for o in range(slabs)] for some in (scales, tangents, pulls, parts)),
            whole,
        )
        return picture(list(zip(image, groups)), (done,)), gradient

    placed = (
        P("depth", None, "width"),
        P("depth", None, "width"),
        P(),
        P(),
        P(),
        P(),
        P(None, ("depth", "width"), None),
    )
    return jax.shard_map(
        on_device,
        mesh=mesh,
        in_specs=placed,
        out_specs=(P(None, ("depth", "width"), None), P("depth", None, "width")),
        check_vma=False,
    )
```

```python
import functools

import jax
import jax.numpy as jnp
from jax import lax
from jax.experimental import pallas as pl
from jax.experimental.pallas import tpu as pltpu
from jax.sharding import PartitionSpec as P

LOG2E = 1.4426950408889634
ROWS = 8
FLOPS_A_US = 1e9
FAR_US, NEAR_US, PULL_US, BLEND_US, TURN_US = 2.4, 0.1, 0, 2.4, 4
COPIES = 8
F32 = jnp.float32

SOOT_STEP, GAS_STEP, PLANCK_STEP, SOURCE, GAS, RATIO = range(6)
KINDS = 6


def smem():
    return pl.BlockSpec(memory_space=pltpu.SMEM)


def vmem():
    return pl.BlockSpec(memory_space=pltpu.VMEM)


def hbm():
    return pl.BlockSpec(memory_space=pltpu.HBM)


def shape(*dims):
    return jax.ShapeDtypeStruct(dims, F32)


def kernel_call(body, name, in_specs, out_specs, out_shape, us=0, mebibytes=4, scratch=()):
    def held(spec):
        return spec.memory_space == pltpu.VMEM

    def placed(spec, out):
        return pltpu.VMEM(out.shape, out.dtype) if held(spec) else out

    if isinstance(out_specs, list):
        out_shape = [placed(spec, out) for spec, out in zip(out_specs, out_shape)]
    else:
        out_shape = placed(out_specs, out_shape)
    def run(*operands, ties=()):
        def untied(*refs):
            return body(*refs[: len(in_specs)], *refs[len(in_specs) + len(ties) :])

        call = pl.pallas_call(
            untied,
            in_specs=[*in_specs, *[pl.BlockSpec(memory_space=pl.ANY)] * len(ties)],
            out_specs=out_specs,
            out_shape=out_shape,
            scratch_shapes=scratch,
            compiler_params=pltpu.CompilerParams(vmem_limit_bytes=mebibytes << 20),
            cost_estimate=pl.CostEstimate(
                flops=int(us * FLOPS_A_US), bytes_accessed=1 << 20, transcendentals=0
            ),
            name=name,
        )
        return call(
            *[
                pltpu.with_memory_space_constraint(x, pltpu.VMEM) if held(spec) else x
                for spec, x in zip(in_specs, operands)
            ],
            *ties,
        )

    return run


def rows_at(tile, count=1):
    return pl.ds(pl.multiple_of(tile * ROWS, count * ROWS), count * ROWS)


def load(soot_rate, gas_rate, planck, order, thermal, soot_share, seed, widths):
    cells, rows, columns = thermal.shape
    bands, lines, _ = seed.shape
    slabs = order.shape[0]
    half = rows // 2
    step = cells // COPIES

    def kernel(
        soot_rate_ref, gas_rate_ref, planck_ref, order_ref, thermal_hbm, soot_hbm, seed_hbm,
        thermal_ref, soot_ref, near_ref, far_ref, const_ref, *cut_refs,
    ):
        *cut_refs, sems = cut_refs
        mine = lax.axis_index("depth")
        copies = []
        for o in range(widths):
            start = pl.multiple_of((lax.axis_index("width") ^ o) * columns, columns)
            copies.append((seed_hbm.at[:, :, pl.ds(start, columns)], cut_refs[o // 2].at[o % 2]))
        for i in range(COPIES):
            part = pl.ds(i * step, step)
            copies.append((thermal_hbm.at[part], thermal_ref.at[part]))
            copies.append((soot_hbm.at[part], soot_ref.at[part]))
        copies = [pltpu.make_async_copy(a, b, sems.at[i]) for i, (a, b) in enumerate(copies)]
        for copy in copies:
            copy.start()

        def tile(value):
            return jnp.full((ROWS, columns), value, F32)

        for b in range(bands):
            gas = tile(gas_rate_ref[b]) * (1.0 / cells)
            wave = tile(planck_ref[b])
            const_ref[SOOT_STEP * bands + b] = tile(soot_rate_ref[b]) * (-LOG2E / cells)
            const_ref[GAS_STEP * bands + b] = gas * -LOG2E
            const_ref[PLANCK_STEP * bands + b] = wave * LOG2E
            const_ref[SOURCE * bands + b] = jnp.exp(wave * 0.5) - 1.0
            const_ref[GAS * bands + b] = gas
            const_ref[RATIO * bands + b] = wave / gas
        for o in range(slabs):
            front = jnp.where(order_ref[mine ^ o] < order_ref[mine], 1.0, 0.0).astype(F32)
            const_ref[KINDS * bands + o] = tile(front)
            const_ref[KINDS * bands + slabs + o] = tile(1.0 - front)
        for copy in copies:
            copy.wait()
        top = mine // (slabs // 2)
        for sums_ref, first in ((near_ref, top), (far_ref, 1 - top)):

            def add(i, _, sums_ref=sums_ref, first=first):
                here = rows_at(first * (half // ROWS) + 2 * i, 2)
                soot = soot_ref[0, here].astype(F32)
                heat = thermal_ref[0, here]
                for k in range(1, cells):
                    soot = soot + soot_ref[k, here].astype(F32)
                    heat = heat + thermal_ref[k, here]
                sums_ref[0, rows_at(2 * i, 2)] = soot
                sums_ref[1, rows_at(2 * i, 2)] = heat
                return 0

            lax.fori_loop(0, half // (2 * ROWS), add, 0)

    return kernel_call(
        kernel,
        "load",
        [smem()] * 4 + [hbm()] * 3,
        [vmem()] * (5 + widths // 2),
        [
            pltpu.VMEM(thermal.shape, thermal.dtype),
            pltpu.VMEM(soot_share.shape, soot_share.dtype),
            shape(2, half, columns),
            shape(2, half, columns),
            shape(KINDS * bands + 2 * slabs, ROWS, columns),
            *[shape(2, bands, lines, columns)] * (widths // 2),
        ],
        us=0,
        mebibytes=52,
        scratch=[pltpu.SemaphoreType.DMA((2 * COPIES + widths,))],
    )(soot_rate, gas_rate, planck, order, thermal, soot_share, seed)


def march(consts, thermal, soot_share, bands, share, o, ties, us):
    cells, _, columns = thermal.shape

    def kernel(const_ref, thermal_ref, soot_ref, part_ref, light_ref):
        first = (lax.axis_index("depth") ^ o) * share

        def tile(i, _):
            here = rows_at(first + 2 * i, 2)

            def const(kind, b):
                one = const_ref[kind * bands + b]
                return jnp.concatenate([one, one], axis=0)

            clear = [None] * bands
            light = [None] * bands
            for k in range(cells):
                heat = thermal_ref[k, here]
                soot = soot_ref[k, here].astype(F32)
                cold = pltpu.reciprocal(heat, approx=True)
                cold2 = cold * cold
                for b in range(bands):
                    fade = jnp.exp2(soot * const(SOOT_STEP, b) + heat * const(GAS_STEP, b))
                    source = pltpu.reciprocal(jnp.exp2(cold * const(PLANCK_STEP, b)) - 1.0, approx=True)
                    if k == 0:
                        beyond = fade
                        emitted = (1.0 - fade) * source
                        local = source
                    else:
                        beyond = clear[b] * fade
                        emitted = (clear[b] - beyond) * source
                        local = clear[b] * source + light[b]
                    part = (emitted + emitted * source) * (cold2 * const(RATIO, b)) + local
                    part_ref[2 * i, k, b] = part[:ROWS]
                    part_ref[2 * i + 1, k, b] = part[ROWS:]
                    light[b] = emitted if k == 0 else light[b] + emitted
                    clear[b] = beyond
            for b in range(bands):
                light_ref[2 * i, b] = light[b][:ROWS]
                light_ref[2 * i + 1, b] = light[b][ROWS:]
            return 0

        lax.fori_loop(0, share // 2, tile, 0)

    return kernel_call(
        kernel,
        "march",
        [vmem()] * 3,
        [vmem()] * 2,
        [shape(share, cells, bands, ROWS, columns), shape(share, bands, ROWS, columns)],
        us=us,
    )(consts, thermal, soot_share, ties=ties)


def turn(sources, targets, ties=(), us=0):
    arrays, names = zip(*sources)
    at = {o: (i, j) for i, held in enumerate(names) for j, o in enumerate(held)}

    def kernel(*refs):
        for target, held in zip(refs[len(arrays) :], targets):
            for j, o in enumerate(held):
                target[j] = refs[at[o][0]][at[o][1]]

    return kernel_call(
        kernel,
        "turn",
        [vmem()] * len(arrays),
        [vmem()] * len(targets),
        [shape(len(held), *arrays[0].shape[1:]) for held in targets],
        us=us,
    )(*arrays, ties=ties)


def join(*terms, ties=()):
    blocks, bands, lines, columns = terms[0].shape

    def kernel(*refs):
        for o in range(blocks):
            total = refs[0][o]
            for ref in refs[1 : len(terms)]:
                total = total + ref[o]
            refs[len(terms) + o % 2][o // 2] = total

    return kernel_call(
        kernel,
        "join",
        [vmem()] * len(terms),
        [vmem()] * 2,
        [shape(blocks // 2, bands, lines, columns)] * 2,
    )(*terms, ties=ties)


def total(terms, ties):
    def kernel(*refs):
        for i in range(terms[0].shape[0]):
            refs[-1][i] = sum((ref[i] for ref in refs[1:-1]), refs[0][i])

    return kernel_call(
        kernel, "total", [vmem()] * len(terms), vmem(), shape(*terms[0].shape)
    )(*terms, ties=ties)


def dim(consts, sums, lights, slabs, twisted, ties):
    share, bands, _, columns = lights[0].shape
    half = len(lights)

    def kernel(const_ref, *refs):
        sum_refs, light_refs = refs[: slabs - 1], refs[slabs - 1 : slabs - 1 + half]
        scale_refs, seen_refs = refs[-2 * half : -half], refs[-half:]
        twist = lax.axis_index("width") if twisted else 0
        for i in range(half):

            def tile(g, _, i=i):
                here = rows_at(((lax.axis_index("depth") ^ i) & (half - 1)) * share + g)
                soot = heat = 0.0
                for j in range(1, slabs):
                    front = const_ref[KINDS * bands + j]
                    soot = soot + sum_refs[j - 1][0, here] * front
                    heat = heat + sum_refs[j - 1][1, here] * front
                for b in range(bands):
                    path = soot * const_ref[SOOT_STEP * bands + b] + heat * const_ref[GAS_STEP * bands + b]
                    scale = const_ref[SOURCE * bands + b] * jnp.exp2(path)
                    scale_refs[i][g, b] = scale
                    seen_refs[i][g ^ twist, b] = light_refs[i][g, b] * scale
                return 0

            lax.fori_loop(0, share, tile, 0)

    outs = kernel_call(
        kernel,
        "dim",
        [vmem()] * (slabs + half),
        [vmem()] * (2 * half),
        [shape(share, bands, ROWS, columns)] * (2 * half),
        us=0,
    )(consts, *sums, *lights, ties=ties)
    return outs[:half], outs[half:]


def pull(consts, seen, tangents, twisted, ties=()):
    slabs = len(seen)
    share, bands, _, columns = seen[0].shape
    half = slabs // 2

    def kernel(const_ref, *refs):
        seen_refs, tangent_refs, pull_ref = refs[:slabs], refs[slabs : 2 * slabs], refs[2 * slabs]
        twist = lax.axis_index("width") if twisted else 0
        for o in range(slabs):

            def tile(i, _, o=o):
                total = None
                for b in range(bands):
                    term = tangent_refs[o][i, b] * seen_refs[o][i, b] * const_ref[GAS * bands + b]
                    total = term if total is None else total + term
                here = rows_at(((lax.axis_index("depth") ^ o) & (half - 1)) * share + (i ^ twist))
                pull_ref[o // half, here] = total
                return 0

            lax.fori_loop(0, share, tile, 0)

    return kernel_call(
        kernel,
        "pull",
        [vmem()] * (1 + 2 * slabs),
        vmem(),
        shape(2, half * share * ROWS, columns),
        us=PULL_US,
    )(consts, *seen, *tangents, ties=ties)


def blend(consts, scales, tangents, pulls, parts, twisted, ties=()):
    slabs = len(parts)
    share, cells, bands, _, columns = parts[0].shape
    half = slabs // 2

    def kernel(const_ref, *refs):
        scale_refs, tangent_refs, pull_refs, part_refs = (
            refs[i * slabs : (i + 1) * slabs] for i in range(4)
        )
        out_hbm, token_ref, gradient_ref, sems = refs[4 * slabs :]
        token_ref[...] = jnp.zeros_like(token_ref)
        mine = lax.axis_index("depth")
        twist = lax.axis_index("width") if twisted else 0
        copies = []
        for o in range(slabs):

            def tile(g, _, o=o):
                here = rows_at(((mine ^ o) & (half - 1)) * share + g)
                weight = [
                    tangent_refs[o][g ^ twist, b] * scale_refs[o][g, b] * const_ref[GAS * bands + b]
                    for b in range(bands)
                ]
                away = None
                for j in range(slabs):
                    side = (o // half) ^ (j // half)
                    term = pull_refs[j][side, here] * const_ref[KINDS * bands + slabs + j]
                    away = term if away is None else away + term
                for k in range(cells):
                    total = part_refs[o][g, k, 0] * weight[0] - away
                    for b in range(1, bands):
                        total = total + part_refs[o][g, k, b] * weight[b]
                    gradient_ref[o, k, rows_at(g)] = total
                return 0

            lax.fori_loop(0, share, tile, 0)
            rows = rows_at((mine ^ o) * share, share)
            copies.append(pltpu.make_async_copy(gradient_ref.at[o], out_hbm.at[:, rows], sems.at[o]))
            copies[-1].start()
        for copy in copies:
            copy.wait()

    height = share * ROWS
    return kernel_call(
        kernel,
        "blend",
        [vmem()] * (1 + 4 * slabs),
        [hbm(), vmem()],
        [shape(cells, slabs * height, columns), shape(ROWS, columns)],
        us=BLEND_US,
        mebibytes=8,
        scratch=[pltpu.VMEM((slabs, cells, height, columns), F32), pltpu.SemaphoreType.DMA((slabs,))],
    )(consts, *scales, *tangents, *pulls, *parts, ties=ties)


def picture(sources, ties=()):
    arrays, names = zip(*sources)
    _, bands, lines, columns = arrays[0].shape
    count = sum(len(held) for held in names)

    def kernel(*refs):
        *block_refs, out_hbm, sems = refs
        copies = []
        for ref, held in zip(block_refs, names):
            for j, o in enumerate(held):
                start = pl.multiple_of((lax.axis_index("width") ^ o) * columns, columns)
                target = out_hbm.at[:, :, pl.ds(start, columns)]
                copies.append(pltpu.make_async_copy(ref.at[j], target, sems.at[o]))
                copies[-1].start()
        for copy in copies:
            copy.wait()

    return kernel_call(
        kernel,
        "picture",
        [vmem()] * len(arrays),
        hbm(),
        shape(bands, lines, count * columns),
        scratch=[pltpu.SemaphoreType.DMA((count,))],
    )(*arrays, ties=ties)


def solution(mesh):
    slabs = mesh.shape["depth"]
    widths = mesh.shape["width"]
    top = slabs // 2
    lower_bits = [1 << i for i in range(top.bit_length() - 1)]
    near, far = range(top), range(top, slabs)

    def swap(value, bit, axis="depth"):
        pairs = [(i, i ^ bit) for i in range(mesh.shape[axis])]
        return lax.ppermute(value, axis, pairs)

    def spread(piece, across=False):
        pieces = {top if across else 0: piece}
        for bit in reversed(lower_bits):
            for o in list(pieces):
                pieces[o ^ bit] = swap(pieces[o], bit)
        return pieces

    def lower(seen):
        kept = dict(enumerate(seen))
        for bit in lower_bits:
            for o in [o for o in kept if o & bit]:
                arrived = swap(kept.pop(o), bit)
                if bit == lower_bits[-1]:
                    return kept[0], arrived
                kept[o ^ bit] = kept[o ^ bit] + arrived

    def on_device(thermal, soot_share, soot_rate, gas_rate, planck, order, seed):
        cells, rows, columns = thermal.shape
        bands, lines, _ = seed.shape
        share = rows // slabs // ROWS
        whole = lines == ROWS

        def twist(blocks):
            at = lax.axis_index("width")
            return jnp.stack([lax.dynamic_index_in_dim(blocks, at ^ o, keepdims=False) for o in range(widths)])

        def to_tiles(blocks):
            if whole:
                return blocks
            lined = twist(blocks).transpose(1, 0, 2, 3).reshape(bands, share, ROWS, columns)
            return lined.transpose(1, 0, 2, 3)

        def to_blocks(*terms, ties=()):
            if whole:
                return join(*terms, ties=ties)
            lined = sum(terms).transpose(1, 0, 2, 3).reshape(bands, widths, lines, columns)
            blocks = twist(lined.transpose(1, 0, 2, 3))
            return blocks[0::2], blocks[1::2]

        parts, lights, scales, seen = {}, {}, {}, {}

        def lit(o, us, *ties):
            parts[o], lights[o] = march(consts, heat, soot, bands, share, o, ties, us)
            return lights[o]

        def dimmed(shares, paths, *ties):
            some = dim(
                consts, [paths[j] for j in range(1, slabs)], [lights[o] for o in shares], slabs, whole, ties
            )
            for i, o in enumerate(shares):
                scales[o], seen[o] = some[0][i], some[1][i]

        evens, odds = range(0, widths, 2), range(1, widths, 2)
        groups = [(o, o + 1) for o in evens]

        def swap_groups(arrays):
            return [arrays[0], *(swap(x, g[0], "width") for x, g in zip(arrays[1:], groups[1:]))]

        heat, soot, near_sums, far_sums, consts, *cut = load(
            soot_rate, gas_rate, planck, order, thermal, soot_share, seed, widths
        )
        across_far = swap(near_sums, top)
        across_near = swap(far_sums, top)
        cut = swap_groups(cut)
        far_paths = spread(far_sums) | spread(across_far, True)
        every, tiles = range(widths), range(share)
        sorted_blocks = [*evens, *odds]

        def side(blocks, s):
            return [(o, s) for o in blocks]

        def both(blocks):
            return side(blocks, 0) + side(blocks, 1)

        done = lit(far[0], FAR_US)
        (mine,) = turn(list(zip(cut, groups)), [sorted_blocks], (done,))
        theirs = swap(mine, top)
        for o in far[1:]:
            done = lit(o, FAR_US, mine, done, across_near)
        dimmed(far, far_paths, done)
        even, odd = turn(
            [(mine, side(sorted_blocks, 0)), (theirs, side(sorted_blocks, 1))],
            [both(evens), both(odds)],
            (seen[far[0]],),
            us=TURN_US,
        )
        odd = swap(odd, 1, "width")
        near_paths = spread(near_sums) | spread(across_near, True)
        cores = [near_paths[o] for o in near_paths if o not in (0, top)]
        seen_far = total(lower([seen[o] for o in far]), (even,))
        across = swap(seen_far, top)
        done = seen_far
        for o in near:
            done = lit(o, NEAR_US, seen_far, done, *(cores if o else ()))
        dimmed(near, near_paths, done)
        seen_near = lower([seen[o] for o in near])
        blocks = turn(
            [(even, both(evens)), (odd, both(odds))], [side(every, 0), side(every, 1)], (seen[near[0]],)
        )
        tangents = spread(to_tiles(blocks[0])) | spread(to_tiles(blocks[1]), True)
        (across,) = turn([(across, tiles)], [tiles], (blocks[0],))
        (across,) = turn([(across, tiles)], [tiles], us=TURN_US)
        image = to_blocks(*seen_near, across)
        odd = swap(image[1], 1, "width")
        pulled = pull(
            consts, [seen[o] for o in range(slabs)], [tangents[o] for o in range(slabs)], whole, (image[0],)
        )
        pulls = {o: swap(pulled, o) if o else pulled for o in range(slabs)}
        image = turn([(image[0], evens), (odd, odds)], groups, (pulled,))
        image = swap_groups(image)
        gradient, done = blend(
            consts,
            *([some[o] for o in range(slabs)] for some in (scales, tangents, pulls, parts)),
            whole,
        )
        return picture(list(zip(image, groups)), (done,)), gradient

    placed = (
        P("depth", None, "width"),
        P("depth", None, "width"),
        P(),
        P(),
        P(),
        P(),
        P(None, ("depth", "width"), None),
    )
    return jax.shard_map(
        on_device,
        mesh=mesh,
        in_specs=placed,
        out_specs=(P(None, ("depth", "width"), None), P("depth", None, "width")),
        check_vma=False,
    )
```

```python
import functools

import jax
import jax.numpy as jnp
from jax import lax
from jax.experimental import pallas as pl
from jax.experimental.pallas import tpu as pltpu
from jax.sharding import PartitionSpec as P

LOG2E = 1.4426950408889634
ROWS = 8
FLOPS_A_US = 1e9
FAR_US, NEAR_US, PULL_US, BLEND_US, TURN_US = 2.4, 0.1, 0, 2.4, 4
COPIES = 8
F32 = jnp.float32

SOOT_STEP, GAS_STEP, PLANCK_STEP, SOURCE, GAS, RATIO = range(6)
KINDS = 6


def smem():
    return pl.BlockSpec(memory_space=pltpu.SMEM)


def vmem():
    return pl.BlockSpec(memory_space=pltpu.VMEM)


def hbm():
    return pl.BlockSpec(memory_space=pltpu.HBM)


def shape(*dims):
    return jax.ShapeDtypeStruct(dims, F32)


def kernel_call(body, name, in_specs, out_specs, out_shape, us=0, mebibytes=4, scratch=()):
    def held(spec):
        return spec.memory_space == pltpu.VMEM

    def placed(spec, out):
        return pltpu.VMEM(out.shape, out.dtype) if held(spec) else out

    if isinstance(out_specs, list):
        out_shape = [placed(spec, out) for spec, out in zip(out_specs, out_shape)]
    else:
        out_shape = placed(out_specs, out_shape)
    def run(*operands, ties=()):
        def untied(*refs):
            return body(*refs[: len(in_specs)], *refs[len(in_specs) + len(ties) :])

        call = pl.pallas_call(
            untied,
            in_specs=[*in_specs, *[pl.BlockSpec(memory_space=pl.ANY)] * len(ties)],
            out_specs=out_specs,
            out_shape=out_shape,
            scratch_shapes=scratch,
            compiler_params=pltpu.CompilerParams(vmem_limit_bytes=mebibytes << 20),
            cost_estimate=pl.CostEstimate(
                flops=int(us * FLOPS_A_US), bytes_accessed=1 << 20, transcendentals=0
            ),
            name=name,
        )
        return call(
            *[
                pltpu.with_memory_space_constraint(x, pltpu.VMEM) if held(spec) else x
                for spec, x in zip(in_specs, operands)
            ],
            *ties,
        )

    return run


def rows_at(tile, count=1):
    return pl.ds(pl.multiple_of(tile * ROWS, count * ROWS), count * ROWS)


def load(soot_rate, gas_rate, planck, order, thermal, soot_share, seed, widths):
    cells, rows, columns = thermal.shape
    bands, lines, _ = seed.shape
    slabs = order.shape[0]
    half = rows // 2
    step = cells // COPIES

    def kernel(
        soot_rate_ref, gas_rate_ref, planck_ref, order_ref, thermal_hbm, soot_hbm, seed_hbm,
        thermal_ref, soot_ref, near_ref, far_ref, const_ref, *cut_refs,
    ):
        *cut_refs, sems = cut_refs
        mine = lax.axis_index("depth")
        copies = []
        for o in range(widths):
            start = pl.multiple_of((lax.axis_index("width") ^ o) * columns, columns)
            copies.append((seed_hbm.at[:, :, pl.ds(start, columns)], cut_refs[o // 2].at[o % 2]))
        for i in range(COPIES):
            part = pl.ds(i * step, step)
            copies.append((thermal_hbm.at[part], thermal_ref.at[part]))
            copies.append((soot_hbm.at[part], soot_ref.at[part]))
        copies = [pltpu.make_async_copy(a, b, sems.at[i]) for i, (a, b) in enumerate(copies)]
        for copy in copies:
            copy.start()

        def tile(value):
            return jnp.full((ROWS, columns), value, F32)

        for b in range(bands):
            gas = tile(gas_rate_ref[b]) * (1.0 / cells)
            wave = tile(planck_ref[b])
            const_ref[SOOT_STEP * bands + b] = tile(soot_rate_ref[b]) * (-LOG2E / cells)
            const_ref[GAS_STEP * bands + b] = gas * -LOG2E
            const_ref[PLANCK_STEP * bands + b] = wave * LOG2E
            const_ref[SOURCE * bands + b] = jnp.exp(wave * 0.5) - 1.0
            const_ref[GAS * bands + b] = gas
            const_ref[RATIO * bands + b] = wave / gas
        for o in range(slabs):
            front = jnp.where(order_ref[mine ^ o] < order_ref[mine], 1.0, 0.0).astype(F32)
            const_ref[KINDS * bands + o] = tile(front)
            const_ref[KINDS * bands + slabs + o] = tile(1.0 - front)
        for copy in copies:
            copy.wait()
        top = mine // (slabs // 2)
        for sums_ref, first in ((near_ref, top), (far_ref, 1 - top)):

            def add(i, _, sums_ref=sums_ref, first=first):
                here = rows_at(first * (half // ROWS) + 2 * i, 2)
                soot = soot_ref[0, here].astype(F32)
                heat = thermal_ref[0, here]
                for k in range(1, cells):
                    soot = soot + soot_ref[k, here].astype(F32)
                    heat = heat + thermal_ref[k, here]
                sums_ref[0, rows_at(2 * i, 2)] = soot
                sums_ref[1, rows_at(2 * i, 2)] = heat
                return 0

            lax.fori_loop(0, half // (2 * ROWS), add, 0)

    return kernel_call(
        kernel,
        "load",
        [smem()] * 4 + [hbm()] * 3,
        [vmem()] * (5 + widths // 2),
        [
            pltpu.VMEM(thermal.shape, thermal.dtype),
            pltpu.VMEM(soot_share.shape, soot_share.dtype),
            shape(2, half, columns),
            shape(2, half, columns),
            shape(KINDS * bands + 2 * slabs, ROWS, columns),
            *[shape(2, bands, lines, columns)] * (widths // 2),
        ],
        us=0,
        mebibytes=52,
        scratch=[pltpu.SemaphoreType.DMA((2 * COPIES + widths,))],
    )(soot_rate, gas_rate, planck, order, thermal, soot_share, seed)


def march(consts, thermal, soot_share, bands, share, o, ties, us):
    cells, _, columns = thermal.shape

    def kernel(const_ref, thermal_ref, soot_ref, fade_ref, source_ref, light_ref):
        first = (lax.axis_index("depth") ^ o) * share

        def tile(i, _):
            here = rows_at(first + 2 * i, 2)

            def const(kind, b):
                one = const_ref[kind * bands + b]
                return jnp.concatenate([one, one], axis=0)

            clear = [None] * bands
            light = [None] * bands
            for k in range(cells):
                heat = thermal_ref[k, here]
                soot = soot_ref[k, here].astype(F32)
                cold = pltpu.reciprocal(heat, approx=True)
                for b in range(bands):
                    fade = jnp.exp2(soot * const(SOOT_STEP, b) + heat * const(GAS_STEP, b))
                    source = pltpu.reciprocal(jnp.exp2(cold * const(PLANCK_STEP, b)) - 1.0, approx=True)
                    fade_ref[2 * i, k, b] = fade[:ROWS]
                    fade_ref[2 * i + 1, k, b] = fade[ROWS:]
                    source_ref[2 * i, k, b] = source[:ROWS]
                    source_ref[2 * i + 1, k, b] = source[ROWS:]
                    if k == 0:
                        light[b] = (1.0 - fade) * source
                        clear[b] = fade
                    else:
                        beyond = clear[b] * fade
                        light[b] = light[b] + (clear[b] - beyond) * source
                        clear[b] = beyond
            for b in range(bands):
                light_ref[2 * i, b] = light[b][:ROWS]
                light_ref[2 * i + 1, b] = light[b][ROWS:]
            return 0

        lax.fori_loop(0, share // 2, tile, 0)

    return kernel_call(
        kernel,
        "march",
        [vmem()] * 3,
        [vmem()] * 3,
        [shape(share, cells, bands, ROWS, columns)] * 2 + [shape(share, bands, ROWS, columns)],
        us=us,
    )(consts, thermal, soot_share, ties=ties)


def turn(sources, targets, ties=(), us=0):
    arrays, names = zip(*sources)
    at = {o: (i, j) for i, held in enumerate(names) for j, o in enumerate(held)}

    def kernel(*refs):
        for target, held in zip(refs[len(arrays) :], targets):
            for j, o in enumerate(held):
                target[j] = refs[at[o][0]][at[o][1]]

    return kernel_call(
        kernel,
        "turn",
        [vmem()] * len(arrays),
        [vmem()] * len(targets),
        [shape(len(held), *arrays[0].shape[1:]) for held in targets],
        us=us,
    )(*arrays, ties=ties)


def join(*terms, ties=()):
    blocks, bands, lines, columns = terms[0].shape

    def kernel(*refs):
        for o in range(blocks):
            total = refs[0][o]
            for ref in refs[1 : len(terms)]:
                total = total + ref[o]
            refs[len(terms) + o % 2][o // 2] = total

    return kernel_call(
        kernel,
        "join",
        [vmem()] * len(terms),
        [vmem()] * 2,
        [shape(blocks // 2, bands, lines, columns)] * 2,
    )(*terms, ties=ties)


def total(terms, ties):
    def kernel(*refs):
        for i in range(terms[0].shape[0]):
            refs[-1][i] = sum((ref[i] for ref in refs[1:-1]), refs[0][i])

    return kernel_call(
        kernel, "total", [vmem()] * len(terms), vmem(), shape(*terms[0].shape)
    )(*terms, ties=ties)


def dim(consts, sums, lights, slabs, twisted, ties):
    share, bands, _, columns = lights[0].shape
    half = len(lights)

    def kernel(const_ref, *refs):
        sum_refs, light_refs = refs[: slabs - 1], refs[slabs - 1 : slabs - 1 + half]
        scale_refs, seen_refs = refs[-2 * half : -half], refs[-half:]
        twist = lax.axis_index("width") if twisted else 0
        for i in range(half):

            def tile(g, _, i=i):
                here = rows_at(((lax.axis_index("depth") ^ i) & (half - 1)) * share + g)
                soot = heat = 0.0
                for j in range(1, slabs):
                    front = const_ref[KINDS * bands + j]
                    soot = soot + sum_refs[j - 1][0, here] * front
                    heat = heat + sum_refs[j - 1][1, here] * front
                for b in range(bands):
                    path = soot * const_ref[SOOT_STEP * bands + b] + heat * const_ref[GAS_STEP * bands + b]
                    scale = const_ref[SOURCE * bands + b] * jnp.exp2(path)
                    scale_refs[i][g, b] = scale
                    seen_refs[i][g ^ twist, b] = light_refs[i][g, b] * scale
                return 0

            lax.fori_loop(0, share, tile, 0)

    outs = kernel_call(
        kernel,
        "dim",
        [vmem()] * (slabs + half),
        [vmem()] * (2 * half),
        [shape(share, bands, ROWS, columns)] * (2 * half),
        us=0,
    )(consts, *sums, *lights, ties=ties)
    return outs[:half], outs[half:]


def pull(consts, seen, tangents, twisted, ties=()):
    slabs = len(seen)
    share, bands, _, columns = seen[0].shape
    half = slabs // 2

    def kernel(const_ref, *refs):
        seen_refs, tangent_refs, pull_ref = refs[:slabs], refs[slabs : 2 * slabs], refs[2 * slabs]
        twist = lax.axis_index("width") if twisted else 0
        for o in range(slabs):

            def tile(i, _, o=o):
                total = None
                for b in range(bands):
                    term = tangent_refs[o][i, b] * seen_refs[o][i, b] * const_ref[GAS * bands + b]
                    total = term if total is None else total + term
                here = rows_at(((lax.axis_index("depth") ^ o) & (half - 1)) * share + (i ^ twist))
                pull_ref[o // half, here] = total
                return 0

            lax.fori_loop(0, share, tile, 0)

    return kernel_call(
        kernel,
        "pull",
        [vmem()] * (1 + 2 * slabs),
        vmem(),
        shape(2, half * share * ROWS, columns),
        us=PULL_US,
    )(consts, *seen, *tangents, ties=ties)


def bend_tile(const_ref, thermal_ref, fade_ref, source_ref, scale_ref, tangent_ref, g, here, twist, store):
    _, cells, bands, _, _ = fade_ref.shape
    clear = [tangent_ref[g ^ twist, b] * scale_ref[g, b] * const_ref[GAS * bands + b] for b in range(bands)]
    passed = None
    for k in range(cells):
        steep = local = emitted = None
        for b in range(bands):
            glow = source_ref[g, k, b]
            beyond = clear[b] * fade_ref[g, k, b]
            given = (clear[b] - beyond) * glow
            slope = (given + given * glow) * const_ref[RATIO * bands + b]
            before = clear[b] * glow
            steep = slope if steep is None else steep + slope
            local = before if local is None else local + before
            emitted = given if emitted is None else emitted + given
            clear[b] = beyond
        cold = pltpu.reciprocal(thermal_ref[k, here], approx=True)
        total = steep * (cold * cold) + local
        store(k, total if passed is None else total + passed)
        passed = emitted if passed is None else passed + emitted


def bend(consts, thermal, fade, source, scale, tangent, o, twisted, ties):
    share, cells, _, _, columns = fade.shape

    def kernel(const_ref, thermal_ref, fade_ref, source_ref, scale_ref, tangent_ref, out_ref):
        first = (lax.axis_index("depth") ^ o) * share
        twist = lax.axis_index("width") if twisted else 0

        def tile(g, _):
            def store(k, value):
                out_ref[k, rows_at(g)] = value

            bend_tile(
                const_ref, thermal_ref, fade_ref, source_ref, scale_ref, tangent_ref,
                g, rows_at(first + g), twist, store,
            )
            return 0

        lax.fori_loop(0, share, tile, 0)

    return kernel_call(
        kernel, "bend", [vmem()] * 6, vmem(), shape(cells, share * ROWS, columns)
    )(consts, thermal, fade, source, scale, tangent, ties=ties)


def blend(consts, thermal, scales, tangents, pulls, fades, sources, bent, twisted, ties=()):
    slabs = len(pulls)
    cells, _, columns = thermal.shape
    share, bands, _, _ = scales[0].shape
    half = slabs // 2
    made = [o for o in range(slabs) if o not in bent]

    def kernel(const_ref, thermal_ref, *refs):
        refs = list(refs)

        def take(names):
            return {o: refs.pop(0) for o in names}

        pull_refs, bent_refs = take(range(slabs)), take(bent)
        scale_refs, tangent_refs, fade_refs, source_refs = (take(made) for _ in range(4))
        out_hbm, token_ref, gradient_ref, sems = refs
        token_ref[...] = jnp.zeros_like(token_ref)
        mine = lax.axis_index("depth")
        twist = lax.axis_index("width") if twisted else 0
        copies = []
        for o in range(slabs):

            def tile(g, _, o=o):
                here = rows_at(((mine ^ o) & (half - 1)) * share + g)
                away = None
                for j in range(slabs):
                    side = (o // half) ^ (j // half)
                    term = pull_refs[j][side, here] * const_ref[KINDS * bands + slabs + j]
                    away = term if away is None else away + term

                def store(k, value):
                    gradient_ref[o, k, rows_at(g)] = value - away

                if o in bent_refs:
                    for k in range(cells):
                        store(k, bent_refs[o][k, rows_at(g)])
                else:
                    bend_tile(
                        const_ref, thermal_ref, fade_refs[o], source_refs[o], scale_refs[o], tangent_refs[o],
                        g, rows_at((mine ^ o) * share + g), twist, store,
                    )
                return 0

            lax.fori_loop(0, share, tile, 0)
            rows = rows_at((mine ^ o) * share, share)
            copies.append(pltpu.make_async_copy(gradient_ref.at[o], out_hbm.at[:, rows], sems.at[o]))
            copies[-1].start()
        for copy in copies:
            copy.wait()

    height = share * ROWS
    operands = [consts, thermal, *pulls, *bent.values()]
    for some in (scales, tangents, fades, sources):
        operands += [some[o] for o in made]
    return kernel_call(
        kernel,
        "blend",
        [vmem()] * len(operands),
        [hbm(), vmem()],
        [shape(cells, slabs * height, columns), shape(ROWS, columns)],
        us=BLEND_US,
        mebibytes=8,
        scratch=[pltpu.VMEM((slabs, cells, height, columns), F32), pltpu.SemaphoreType.DMA((slabs,))],
    )(*operands, ties=ties)


def picture(sources, ties=()):
    arrays, names = zip(*sources)
    _, bands, lines, columns = arrays[0].shape
    count = sum(len(held) for held in names)

    def kernel(*refs):
        *block_refs, out_hbm, sems = refs
        copies = []
        for ref, held in zip(block_refs, names):
            for j, o in enumerate(held):
                start = pl.multiple_of((lax.axis_index("width") ^ o) * columns, columns)
                target = out_hbm.at[:, :, pl.ds(start, columns)]
                copies.append(pltpu.make_async_copy(ref.at[j], target, sems.at[o]))
                copies[-1].start()
        for copy in copies:
            copy.wait()

    return kernel_call(
        kernel,
        "picture",
        [vmem()] * len(arrays),
        hbm(),
        shape(bands, lines, count * columns),
        scratch=[pltpu.SemaphoreType.DMA((count,))],
    )(*arrays, ties=ties)


def solution(mesh):
    slabs = mesh.shape["depth"]
    widths = mesh.shape["width"]
    top = slabs // 2
    lower_bits = [1 << i for i in range(top.bit_length() - 1)]
    near, far = range(top), range(top, slabs)

    def swap(value, bit, axis="depth"):
        pairs = [(i, i ^ bit) for i in range(mesh.shape[axis])]
        return lax.ppermute(value, axis, pairs)

    def spread(piece, across=False):
        pieces = {top if across else 0: piece}
        for bit in reversed(lower_bits):
            for o in list(pieces):
                pieces[o ^ bit] = swap(pieces[o], bit)
        return pieces

    def lower(seen):
        kept = dict(enumerate(seen))
        for bit in lower_bits:
            for o in [o for o in kept if o & bit]:
                arrived = swap(kept.pop(o), bit)
                if bit == lower_bits[-1]:
                    return kept[0], arrived
                kept[o ^ bit] = kept[o ^ bit] + arrived

    def on_device(thermal, soot_share, soot_rate, gas_rate, planck, order, seed):
        cells, rows, columns = thermal.shape
        bands, lines, _ = seed.shape
        share = rows // slabs // ROWS
        whole = lines == ROWS

        def twist(blocks):
            at = lax.axis_index("width")
            return jnp.stack([lax.dynamic_index_in_dim(blocks, at ^ o, keepdims=False) for o in range(widths)])

        def to_tiles(blocks):
            if whole:
                return blocks
            lined = twist(blocks).transpose(1, 0, 2, 3).reshape(bands, share, ROWS, columns)
            return lined.transpose(1, 0, 2, 3)

        def to_blocks(*terms, ties=()):
            if whole:
                return join(*terms, ties=ties)
            lined = sum(terms).transpose(1, 0, 2, 3).reshape(bands, widths, lines, columns)
            blocks = twist(lined.transpose(1, 0, 2, 3))
            return blocks[0::2], blocks[1::2]

        fades, sources, lights, scales, seen = {}, {}, {}, {}, {}

        def lit(o, us, *ties):
            fades[o], sources[o], lights[o] = march(consts, heat, soot, bands, share, o, ties, us)
            return lights[o]

        def dimmed(shares, paths, *ties):
            some = dim(
                consts, [paths[j] for j in range(1, slabs)], [lights[o] for o in shares], slabs, whole, ties
            )
            for i, o in enumerate(shares):
                scales[o], seen[o] = some[0][i], some[1][i]

        evens, odds = range(0, widths, 2), range(1, widths, 2)
        groups = [(o, o + 1) for o in evens]

        def swap_groups(arrays):
            return [arrays[0], *(swap(x, g[0], "width") for x, g in zip(arrays[1:], groups[1:]))]

        heat, soot, near_sums, far_sums, consts, *cut = load(
            soot_rate, gas_rate, planck, order, thermal, soot_share, seed, widths
        )
        across_far = swap(near_sums, top)
        across_near = swap(far_sums, top)
        cut = swap_groups(cut)
        far_paths = spread(far_sums) | spread(across_far, True)
        every, tiles = range(widths), range(share)
        sorted_blocks = [*evens, *odds]

        def side(blocks, s):
            return [(o, s) for o in blocks]

        def both(blocks):
            return side(blocks, 0) + side(blocks, 1)

        done = lit(far[0], FAR_US)
        (mine,) = turn(list(zip(cut, groups)), [sorted_blocks], (done,))
        theirs = swap(mine, top)
        for o in far[1:]:
            done = lit(o, FAR_US, mine, done, across_near)
        dimmed(far, far_paths, done)
        even, odd = turn(
            [(mine, side(sorted_blocks, 0)), (theirs, side(sorted_blocks, 1))],
            [both(evens), both(odds)],
            (seen[far[0]],),
            us=TURN_US,
        )
        odd = swap(odd, 1, "width")
        near_paths = spread(near_sums) | spread(across_near, True)
        cores = [near_paths[o] for o in near_paths if o not in (0, top)]
        seen_far = total(lower([seen[o] for o in far]), (even, *cores))
        across = swap(seen_far, top)
        done = seen_far
        for o in near:
            done = lit(o, NEAR_US, seen_far, done)
        dimmed(near, near_paths, done)
        seen_near = lower([seen[o] for o in near])
        blocks = turn(
            [(even, both(evens)), (odd, both(odds))], [side(every, 0), side(every, 1)], (seen[near[0]],)
        )
        tangents = spread(to_tiles(blocks[0])) | spread(to_tiles(blocks[1]), True)
        (across,) = turn([(across, tiles)], [tiles], (blocks[0],))
        (across,) = turn([(across, tiles)], [tiles], us=TURN_US)
        image = to_blocks(*seen_near, across)
        odd = swap(image[1], 1, "width")
        pulled = pull(
            consts, [seen[o] for o in range(slabs)], [tangents[o] for o in range(slabs)], whole, (image[0],)
        )
        pulls = {o: swap(pulled, o) if o else pulled for o in range(slabs)}
        bent = {
            o: bend(consts, heat, fades[o], sources[o], scales[o], tangents[o], o, whole, (pulled,))
            for o in near[:1]
        }
        image = turn([(image[0], evens), (odd, odds)], groups, tuple(bent.values()))
        image = swap_groups(image)
        gradient, done = blend(
            consts, heat, scales, tangents, [pulls[o] for o in range(slabs)], fades, sources, bent, whole
        )
        return picture(list(zip(image, groups)), (done,)), gradient

    placed = (
        P("depth", None, "width"),
        P("depth", None, "width"),
        P(),
        P(),
        P(),
        P(),
        P(None, ("depth", "width"), None),
    )
    return jax.shard_map(
        on_device,
        mesh=mesh,
        in_specs=placed,
        out_specs=(P(None, ("depth", "width"), None), P("depth", None, "width")),
        check_vma=False,
    )
```

```python
import functools

import jax
import jax.numpy as jnp
from jax import lax
from jax.experimental import pallas as pl
from jax.experimental.pallas import tpu as pltpu
from jax.sharding import PartitionSpec as P

LOG2E = 1.4426950408889634
ROWS = 8
FLOPS_A_US = 1e9
FAR_US, NEAR_US, PULL_US, BLEND_US, TURN_US = 2.4, 0.1, 0, 2.4, 4
COPIES = 8
F32 = jnp.float32

SOOT_STEP, GAS_STEP, PLANCK_STEP, SOURCE, GAS, RATIO = range(6)
KINDS = 6


def smem():
    return pl.BlockSpec(memory_space=pltpu.SMEM)


def vmem():
    return pl.BlockSpec(memory_space=pltpu.VMEM)


def hbm():
    return pl.BlockSpec(memory_space=pltpu.HBM)


def shape(*dims):
    return jax.ShapeDtypeStruct(dims, F32)


def kernel_call(body, name, in_specs, out_specs, out_shape, us=0, mebibytes=4, scratch=()):
    def held(spec):
        return spec.memory_space == pltpu.VMEM

    def placed(spec, out):
        return pltpu.VMEM(out.shape, out.dtype) if held(spec) else out

    if isinstance(out_specs, list):
        out_shape = [placed(spec, out) for spec, out in zip(out_specs, out_shape)]
    else:
        out_shape = placed(out_specs, out_shape)
    def run(*operands, ties=()):
        def untied(*refs):
            return body(*refs[: len(in_specs)], *refs[len(in_specs) + len(ties) :])

        call = pl.pallas_call(
            untied,
            in_specs=[*in_specs, *[pl.BlockSpec(memory_space=pl.ANY)] * len(ties)],
            out_specs=out_specs,
            out_shape=out_shape,
            scratch_shapes=scratch,
            compiler_params=pltpu.CompilerParams(vmem_limit_bytes=mebibytes << 20),
            cost_estimate=pl.CostEstimate(
                flops=int(us * FLOPS_A_US), bytes_accessed=1 << 20, transcendentals=0
            ),
            name=name,
        )
        return call(
            *[
                pltpu.with_memory_space_constraint(x, pltpu.VMEM) if held(spec) else x
                for spec, x in zip(in_specs, operands)
            ],
            *ties,
        )

    return run


def rows_at(tile, count=1):
    return pl.ds(pl.multiple_of(tile * ROWS, count * ROWS), count * ROWS)


def load(soot_rate, gas_rate, planck, order, thermal, soot_share, seed, widths):
    cells, rows, columns = thermal.shape
    bands, lines, _ = seed.shape
    slabs = order.shape[0]
    half = rows // 2
    step = cells // COPIES

    def kernel(
        soot_rate_ref, gas_rate_ref, planck_ref, order_ref, thermal_hbm, soot_hbm, seed_hbm,
        thermal_ref, soot_ref, near_ref, far_ref, const_ref, *cut_refs,
    ):
        *cut_refs, sems = cut_refs
        mine = lax.axis_index("depth")
        copies = []
        for o in range(widths):
            start = pl.multiple_of((lax.axis_index("width") ^ o) * columns, columns)
            copies.append((seed_hbm.at[:, :, pl.ds(start, columns)], cut_refs[o // 2].at[o % 2]))
        for i in range(COPIES):
            part = pl.ds(i * step, step)
            copies.append((thermal_hbm.at[part], thermal_ref.at[part]))
            copies.append((soot_hbm.at[part], soot_ref.at[part]))
        copies = [pltpu.make_async_copy(a, b, sems.at[i]) for i, (a, b) in enumerate(copies)]
        for copy in copies:
            copy.start()

        def tile(value):
            return jnp.full((ROWS, columns), value, F32)

        for b in range(bands):
            gas = tile(gas_rate_ref[b]) * (1.0 / cells)
            wave = tile(planck_ref[b])
            const_ref[SOOT_STEP * bands + b] = tile(soot_rate_ref[b]) * (-LOG2E / cells)
            const_ref[GAS_STEP * bands + b] = gas * -LOG2E
            const_ref[PLANCK_STEP * bands + b] = wave * LOG2E
            const_ref[SOURCE * bands + b] = jnp.exp(wave * 0.5) - 1.0
            const_ref[GAS * bands + b] = gas
            const_ref[RATIO * bands + b] = wave / gas
        for o in range(slabs):
            front = jnp.where(order_ref[mine ^ o] < order_ref[mine], 1.0, 0.0).astype(F32)
            const_ref[KINDS * bands + o] = tile(front)
            const_ref[KINDS * bands + slabs + o] = tile(1.0 - front)
        for copy in copies:
            copy.wait()
        top = mine // (slabs // 2)
        for sums_ref, first in ((near_ref, top), (far_ref, 1 - top)):

            def add(i, _, sums_ref=sums_ref, first=first):
                here = rows_at(first * (half // ROWS) + 2 * i, 2)
                soot = soot_ref[0, here].astype(F32)
                heat = thermal_ref[0, here]
                for k in range(1, cells):
                    soot = soot + soot_ref[k, here].astype(F32)
                    heat = heat + thermal_ref[k, here]
                sums_ref[0, rows_at(2 * i, 2)] = soot
                sums_ref[1, rows_at(2 * i, 2)] = heat
                return 0

            lax.fori_loop(0, half // (2 * ROWS), add, 0)

    return kernel_call(
        kernel,
        "load",
        [smem()] * 4 + [hbm()] * 3,
        [vmem()] * (5 + widths // 2),
        [
            pltpu.VMEM(thermal.shape, thermal.dtype),
            pltpu.VMEM(soot_share.shape, soot_share.dtype),
            shape(2, half, columns),
            shape(2, half, columns),
            shape(KINDS * bands + 2 * slabs, ROWS, columns),
            *[shape(2, bands, lines, columns)] * (widths // 2),
        ],
        us=0,
        mebibytes=52,
        scratch=[pltpu.SemaphoreType.DMA((2 * COPIES + widths,))],
    )(soot_rate, gas_rate, planck, order, thermal, soot_share, seed)


def march(consts, thermal, soot_share, bands, share, o, ties, us):
    cells, _, columns = thermal.shape

    def kernel(const_ref, thermal_ref, soot_ref, fade_ref, source_ref, light_ref):
        first = (lax.axis_index("depth") ^ o) * share

        def tile(i, _):
            here = rows_at(first + 2 * i, 2)

            def const(kind, b):
                one = const_ref[kind * bands + b]
                return jnp.concatenate([one, one], axis=0)

            clear = [None] * bands
            light = [None] * bands
            for k in range(cells):
                heat = thermal_ref[k, here]
                soot = soot_ref[k, here].astype(F32)
                cold = pltpu.reciprocal(heat, approx=True)
                glow = []
                for b in range(0, bands, 2):
                    x, y = (jnp.exp2(cold * const(PLANCK_STEP, b + i)) - 1.0 for i in range(2))
                    inverse = pltpu.reciprocal(x * y, approx=True)
                    glow += [y * inverse, x * inverse]
                for b in range(bands):
                    fade = jnp.exp2(soot * const(SOOT_STEP, b) + heat * const(GAS_STEP, b))
                    source = glow[b]
                    fade_ref[2 * i, k, b] = fade[:ROWS]
                    fade_ref[2 * i + 1, k, b] = fade[ROWS:]
                    source_ref[2 * i, k, b] = source[:ROWS]
                    source_ref[2 * i + 1, k, b] = source[ROWS:]
                    if k == 0:
                        light[b] = (1.0 - fade) * source
                        clear[b] = fade
                    else:
                        beyond = clear[b] * fade
                        light[b] = light[b] + (clear[b] - beyond) * source
                        clear[b] = beyond
            for b in range(bands):
                light_ref[2 * i, b] = light[b][:ROWS]
                light_ref[2 * i + 1, b] = light[b][ROWS:]
            return 0

        lax.fori_loop(0, share // 2, tile, 0)

    return kernel_call(
        kernel,
        "march",
        [vmem()] * 3,
        [vmem()] * 3,
        [shape(share, cells, bands, ROWS, columns)] * 2 + [shape(share, bands, ROWS, columns)],
        us=us,
    )(consts, thermal, soot_share, ties=ties)


def turn(sources, targets, ties=(), us=0):
    arrays, names = zip(*sources)
    at = {o: (i, j) for i, held in enumerate(names) for j, o in enumerate(held)}

    def kernel(*refs):
        for target, held in zip(refs[len(arrays) :], targets):
            for j, o in enumerate(held):
                target[j] = refs[at[o][0]][at[o][1]]

    return kernel_call(
        kernel,
        "turn",
        [vmem()] * len(arrays),
        [vmem()] * len(targets),
        [shape(len(held), *arrays[0].shape[1:]) for held in targets],
        us=us,
    )(*arrays, ties=ties)


def join(*terms, ties=()):
    blocks, bands, lines, columns = terms[0].shape

    def kernel(*refs):
        for o in range(blocks):
            total = refs[0][o]
            for ref in refs[1 : len(terms)]:
                total = total + ref[o]
            refs[len(terms) + o % 2][o // 2] = total

    return kernel_call(
        kernel,
        "join",
        [vmem()] * len(terms),
        [vmem()] * 2,
        [shape(blocks // 2, bands, lines, columns)] * 2,
    )(*terms, ties=ties)


def total(terms, ties):
    def kernel(*refs):
        for i in range(terms[0].shape[0]):
            refs[-1][i] = sum((ref[i] for ref in refs[1:-1]), refs[0][i])

    return kernel_call(
        kernel, "total", [vmem()] * len(terms), vmem(), shape(*terms[0].shape)
    )(*terms, ties=ties)


def dim(consts, sums, lights, slabs, twisted, ties):
    share, bands, _, columns = lights[0].shape
    half = len(lights)

    def kernel(const_ref, *refs):
        sum_refs, light_refs = refs[: slabs - 1], refs[slabs - 1 : slabs - 1 + half]
        scale_refs, seen_refs = refs[-2 * half : -half], refs[-half:]
        twist = lax.axis_index("width") if twisted else 0
        for i in range(half):

            def tile(g, _, i=i):
                here = rows_at(((lax.axis_index("depth") ^ i) & (half - 1)) * share + g)
                soot = heat = 0.0
                for j in range(1, slabs):
                    front = const_ref[KINDS * bands + j]
                    soot = soot + sum_refs[j - 1][0, here] * front
                    heat = heat + sum_refs[j - 1][1, here] * front
                for b in range(bands):
                    path = soot * const_ref[SOOT_STEP * bands + b] + heat * const_ref[GAS_STEP * bands + b]
                    scale = const_ref[SOURCE * bands + b] * jnp.exp2(path)
                    scale_refs[i][g, b] = scale
                    seen_refs[i][g ^ twist, b] = light_refs[i][g, b] * scale
                return 0

            lax.fori_loop(0, share, tile, 0)

    outs = kernel_call(
        kernel,
        "dim",
        [vmem()] * (slabs + half),
        [vmem()] * (2 * half),
        [shape(share, bands, ROWS, columns)] * (2 * half),
        us=0,
    )(consts, *sums, *lights, ties=ties)
    return outs[:half], outs[half:]


def pull(consts, seen, tangents, twisted, ties=()):
    slabs = len(seen)
    share, bands, _, columns = seen[0].shape
    half = slabs // 2

    def kernel(const_ref, *refs):
        seen_refs, tangent_refs, pull_ref = refs[:slabs], refs[slabs : 2 * slabs], refs[2 * slabs]
        twist = lax.axis_index("width") if twisted else 0
        for o in range(slabs):

            def tile(i, _, o=o):
                total = None
                for b in range(bands):
                    term = tangent_refs[o][i, b] * seen_refs[o][i, b] * const_ref[GAS * bands + b]
                    total = term if total is None else total + term
                here = rows_at(((lax.axis_index("depth") ^ o) & (half - 1)) * share + (i ^ twist))
                pull_ref[o // half, here] = total
                return 0

            lax.fori_loop(0, share, tile, 0)

    return kernel_call(
        kernel,
        "pull",
        [vmem()] * (1 + 2 * slabs),
        vmem(),
        shape(2, half * share * ROWS, columns),
        us=PULL_US,
    )(consts, *seen, *tangents, ties=ties)


def bend_tile(const_ref, thermal_ref, fade_ref, source_ref, scale_ref, tangent_ref, g, here, twist, store):
    _, cells, bands, _, _ = fade_ref.shape
    clear = [tangent_ref[g ^ twist, b] * scale_ref[g, b] * const_ref[GAS * bands + b] for b in range(bands)]
    passed = None
    for k in range(cells):
        steep = local = emitted = None
        for b in range(bands):
            glow = source_ref[g, k, b]
            beyond = clear[b] * fade_ref[g, k, b]
            given = (clear[b] - beyond) * glow
            slope = (given + given * glow) * const_ref[RATIO * bands + b]
            before = clear[b] * glow
            steep = slope if steep is None else steep + slope
            local = before if local is None else local + before
            emitted = given if emitted is None else emitted + given
            clear[b] = beyond
        cold = pltpu.reciprocal(thermal_ref[k, here], approx=True)
        total = steep * (cold * cold) + local
        store(k, total if passed is None else total + passed)
        passed = emitted if passed is None else passed + emitted


def bend(consts, thermal, fade, source, scale, tangent, o, twisted, ties):
    share, cells, _, _, columns = fade.shape

    def kernel(const_ref, thermal_ref, fade_ref, source_ref, scale_ref, tangent_ref, out_ref):
        first = (lax.axis_index("depth") ^ o) * share
        twist = lax.axis_index("width") if twisted else 0

        def tile(g, _):
            def store(k, value):
                out_ref[k, rows_at(g)] = value

            bend_tile(
                const_ref, thermal_ref, fade_ref, source_ref, scale_ref, tangent_ref,
                g, rows_at(first + g), twist, store,
            )
            return 0

        lax.fori_loop(0, share, tile, 0)

    return kernel_call(
        kernel, "bend", [vmem()] * 6, vmem(), shape(cells, share * ROWS, columns)
    )(consts, thermal, fade, source, scale, tangent, ties=ties)


def blend(consts, thermal, scales, tangents, pulls, fades, sources, bent, twisted, ties=()):
    slabs = len(pulls)
    cells, _, columns = thermal.shape
    share, bands, _, _ = scales[0].shape
    half = slabs // 2
    made = [o for o in range(slabs) if o not in bent]

    def kernel(const_ref, thermal_ref, *refs):
        refs = list(refs)

        def take(names):
            return {o: refs.pop(0) for o in names}

        pull_refs, bent_refs = take(range(slabs)), take(bent)
        scale_refs, tangent_refs, fade_refs, source_refs = (take(made) for _ in range(4))
        out_hbm, token_ref, gradient_ref, sems = refs
        token_ref[...] = jnp.zeros_like(token_ref)
        mine = lax.axis_index("depth")
        twist = lax.axis_index("width") if twisted else 0
        copies = []
        for o in range(slabs):

            def tile(g, _, o=o):
                here = rows_at(((mine ^ o) & (half - 1)) * share + g)
                away = None
                for j in range(slabs):
                    side = (o // half) ^ (j // half)
                    term = pull_refs[j][side, here] * const_ref[KINDS * bands + slabs + j]
                    away = term if away is None else away + term

                def store(k, value):
                    gradient_ref[o, k, rows_at(g)] = value - away

                if o in bent_refs:
                    for k in range(cells):
                        store(k, bent_refs[o][k, rows_at(g)])
                else:
                    bend_tile(
                        const_ref, thermal_ref, fade_refs[o], source_refs[o], scale_refs[o], tangent_refs[o],
                        g, rows_at((mine ^ o) * share + g), twist, store,
                    )
                return 0

            lax.fori_loop(0, share, tile, 0)
            rows = rows_at((mine ^ o) * share, share)
            copies.append(pltpu.make_async_copy(gradient_ref.at[o], out_hbm.at[:, rows], sems.at[o]))
            copies[-1].start()
        for copy in copies:
            copy.wait()

    height = share * ROWS
    operands = [consts, thermal, *pulls, *bent.values()]
    for some in (scales, tangents, fades, sources):
        operands += [some[o] for o in made]
    return kernel_call(
        kernel,
        "blend",
        [vmem()] * len(operands),
        [hbm(), vmem()],
        [shape(cells, slabs * height, columns), shape(ROWS, columns)],
        us=BLEND_US,
        mebibytes=8,
        scratch=[pltpu.VMEM((slabs, cells, height, columns), F32), pltpu.SemaphoreType.DMA((slabs,))],
    )(*operands, ties=ties)


def picture(sources, ties=()):
    arrays, names = zip(*sources)
    _, bands, lines, columns = arrays[0].shape
    count = sum(len(held) for held in names)

    def kernel(*refs):
        *block_refs, out_hbm, sems = refs
        copies = []
        for ref, held in zip(block_refs, names):
            for j, o in enumerate(held):
                start = pl.multiple_of((lax.axis_index("width") ^ o) * columns, columns)
                target = out_hbm.at[:, :, pl.ds(start, columns)]
                copies.append(pltpu.make_async_copy(ref.at[j], target, sems.at[o]))
                copies[-1].start()
        for copy in copies:
            copy.wait()

    return kernel_call(
        kernel,
        "picture",
        [vmem()] * len(arrays),
        hbm(),
        shape(bands, lines, count * columns),
        scratch=[pltpu.SemaphoreType.DMA((count,))],
    )(*arrays, ties=ties)


def solution(mesh):
    slabs = mesh.shape["depth"]
    widths = mesh.shape["width"]
    top = slabs // 2
    lower_bits = [1 << i for i in range(top.bit_length() - 1)]
    near, far = range(top), range(top, slabs)

    def swap(value, bit, axis="depth"):
        pairs = [(i, i ^ bit) for i in range(mesh.shape[axis])]
        return lax.ppermute(value, axis, pairs)

    def spread(piece, across=False):
        pieces = {top if across else 0: piece}
        for bit in reversed(lower_bits):
            for o in list(pieces):
                pieces[o ^ bit] = swap(pieces[o], bit)
        return pieces

    def lower(seen):
        kept = dict(enumerate(seen))
        for bit in lower_bits:
            for o in [o for o in kept if o & bit]:
                arrived = swap(kept.pop(o), bit)
                if bit == lower_bits[-1]:
                    return kept[0], arrived
                kept[o ^ bit] = kept[o ^ bit] + arrived

    def on_device(thermal, soot_share, soot_rate, gas_rate, planck, order, seed):
        cells, rows, columns = thermal.shape
        bands, lines, _ = seed.shape
        share = rows // slabs // ROWS
        whole = lines == ROWS

        def twist(blocks):
            at = lax.axis_index("width")
            return jnp.stack([lax.dynamic_index_in_dim(blocks, at ^ o, keepdims=False) for o in range(widths)])

        def to_tiles(blocks):
            if whole:
                return blocks
            lined = twist(blocks).transpose(1, 0, 2, 3).reshape(bands, share, ROWS, columns)
            return lined.transpose(1, 0, 2, 3)

        def to_blocks(*terms, ties=()):
            if whole:
                return join(*terms, ties=ties)
            lined = sum(terms).transpose(1, 0, 2, 3).reshape(bands, widths, lines, columns)
            blocks = twist(lined.transpose(1, 0, 2, 3))
            return blocks[0::2], blocks[1::2]

        fades, sources, lights, scales, seen = {}, {}, {}, {}, {}

        def lit(o, us, *ties):
            fades[o], sources[o], lights[o] = march(consts, heat, soot, bands, share, o, ties, us)
            return lights[o]

        def dimmed(shares, paths, *ties):
            some = dim(
                consts, [paths[j] for j in range(1, slabs)], [lights[o] for o in shares], slabs, whole, ties
            )
            for i, o in enumerate(shares):
                scales[o], seen[o] = some[0][i], some[1][i]

        evens, odds = range(0, widths, 2), range(1, widths, 2)
        groups = [(o, o + 1) for o in evens]

        def swap_groups(arrays):
            return [arrays[0], *(swap(x, g[0], "width") for x, g in zip(arrays[1:], groups[1:]))]

        heat, soot, near_sums, far_sums, consts, *cut = load(
            soot_rate, gas_rate, planck, order, thermal, soot_share, seed, widths
        )
        across_far = swap(near_sums, top)
        across_near = swap(far_sums, top)
        cut = swap_groups(cut)
        far_paths = spread(far_sums) | spread(across_far, True)
        every, tiles = range(widths), range(share)
        sorted_blocks = [*evens, *odds]

        def side(blocks, s):
            return [(o, s) for o in blocks]

        def both(blocks):
            return side(blocks, 0) + side(blocks, 1)

        done = lit(far[0], FAR_US)
        (mine,) = turn(list(zip(cut, groups)), [sorted_blocks], (done,))
        theirs = swap(mine, top)
        for o in far[1:]:
            done = lit(o, FAR_US, mine, done, across_near)
        dimmed(far, far_paths, done)
        even, odd = turn(
            [(mine, side(sorted_blocks, 0)), (theirs, side(sorted_blocks, 1))],
            [both(evens), both(odds)],
            (seen[far[0]],),
            us=TURN_US,
        )
        odd = swap(odd, 1, "width")
        near_paths = spread(near_sums) | spread(across_near, True)
        cores = [near_paths[o] for o in near_paths if o not in (0, top)]
        seen_far = total(lower([seen[o] for o in far]), (even, *cores))
        across = swap(seen_far, top)
        done = seen_far
        for o in near:
            done = lit(o, NEAR_US, seen_far, done)
        dimmed(near, near_paths, done)
        seen_near = lower([seen[o] for o in near])
        blocks = turn(
            [(even, both(evens)), (odd, both(odds))], [side(every, 0), side(every, 1)], (seen[near[0]],)
        )
        tangents = spread(to_tiles(blocks[0])) | spread(to_tiles(blocks[1]), True)
        (across,) = turn([(across, tiles)], [tiles], (blocks[0],))
        (across,) = turn([(across, tiles)], [tiles], us=TURN_US)
        image = to_blocks(*seen_near, across)
        odd = swap(image[1], 1, "width")
        pulled = pull(
            consts, [seen[o] for o in range(slabs)], [tangents[o] for o in range(slabs)], whole, (image[0],)
        )
        pulls = {o: swap(pulled, o) if o else pulled for o in range(slabs)}
        bent = {
            o: bend(consts, heat, fades[o], sources[o], scales[o], tangents[o], o, whole, (pulled,))
            for o in near[:1]
        }
        image = turn([(image[0], evens), (odd, odds)], groups, tuple(bent.values()))
        image = swap_groups(image)
        gradient, done = blend(
            consts, heat, scales, tangents, [pulls[o] for o in range(slabs)], fades, sources, bent, whole
        )
        return picture(list(zip(image, groups)), (done,)), gradient

    placed = (
        P("depth", None, "width"),
        P("depth", None, "width"),
        P(),
        P(),
        P(),
        P(),
        P(None, ("depth", "width"), None),
    )
    return jax.shard_map(
        on_device,
        mesh=mesh,
        in_specs=placed,
        out_specs=(P(None, ("depth", "width"), None), P("depth", None, "width")),
        check_vma=False,
    )
```
